256 devices in a mesh: gx: 16 (over z_lo, x), gy: 8 (over y, z_hi), gz: 2 (over core).
Axes of the slice: x: 4, y: 4, z: 8 (z_hi: 2, z_lo: 4; z = z_hi * 4 + z_lo), core: 2. Of those that a mesh axis runs over, the one named last changes fastest.
Arguments:
- state_field: float32 [256, 5, 128, 256], P('gx', None, 'gy', 'gz'), may hold values from -6 to 6
- source: float32 [256, 5, 128, 256], P('gx', None, 'gy', 'gz'), may hold values from -6 to 6
- fluid_mask: int32 [256, 128, 256], P('gx', 'gy', 'gz'), may hold values 0 or 1
- cell_kind: int32 [256, 128, 256], P('gx', 'gy', 'gz'), may hold values from 0 to 2
- boundary_side_number: int32 [256, 128, 256], P('gx', 'gy', 'gz'), may hold values from 0 to 11
- center_matrix: float32 [5, 5], replicated, may hold values from -2.5 to 2.5
- flux_jacobian_blocks: float32 [6, 5, 5], replicated, may hold values from -1 to 1
- wall_matrix: float32 [5, 5], replicated, may hold values from -2.5 to 2.5
- diag_inverse: float32 [256, 5, 5, 128, 256], P('gx', None, None, 'gy', 'gz'), may hold values from -0.01 to 0.1
- lower_coupling: float32 [5, 5], replicated, may hold values from -10 to 10
- upper_neighbour_block: float32 [5, 5], replicated, may hold values from -10 to 10
Outputs:
- update: float32 [256, 5, 128, 256], P('gx', None, 'gy', 'gz')
- residual: float32 [256, 5, 128, 256], P('gx', None, 'gy', 'gz')
The draws below stay inside these ranges and needn't reach their ends.
Inputs may be any that keep to these rules, and one draw needn't show every extreme that they name: `boundary_side_number`: values 0 to 5 name the face of a cell that is a wall (lower x, upper x, lower y, upper y, lower z, upper z); 6 or more: no wall face. `cell_kind`: 0 full cell, 1 cut cell, 2 small cut cell.
All inputs are finite; a program needn't handle non-finite values. No bound on the sum of `fluid_mask` on one device may be relied on, other than what follows from the above.
Results may differ from the reference program's by a relative error of at most 0.00018.
Values sent between devices are 32-bit elements; how exact they have to be, the bound alone decides.
A program may use at most 64 MiB of HBM per device.

```python
import jax
import jax.numpy as jnp
from jax import lax

COMP = 5
MESH_SPAN_EAST = 256
NY = 128
NZ = 256


def draw_diag_inverse(key, part):
    key_jitter = jax.random.fold_in(key, 11)
    seed_position = jax.random.fold_in(key, 12)
    key_depth = jax.random.fold_in(key, 13)
    jitter = jnp.clip(0.03 * jax.random.normal(key_jitter, (MESH_SPAN_EAST, 5, 5, NY, NZ), jnp.float32), -0.1, 0.1)
    packet_bundles = jax.random.randint(seed_position, (3,), 0, MESH_SPAN_EAST)
    nesting_tiers = jax.random.uniform(key_depth, (3,), jnp.float32, 0.6, 0.85)
    vertical_strip = jnp.arange(MESH_SPAN_EAST)
    magnitude_multiplier = jnp.prod(jnp.where(vertical_strip[:, None] == packet_bundles[None, :], nesting_tiers[None, :], 1.0), axis=1)
    identity = jnp.eye(5, dtype=jnp.float32)
    offdiag = jitter * (1.0 - identity)[None, :, :, None, None]
    return 0.1 * (identity[None, :, :, None, None] * magnitude_multiplier[:, None, None, None, None] + offdiag)


def plane_rotation(size, first, second, angle):
    identity = jnp.eye(size, dtype=jnp.float32)
    cosine = jnp.cos(angle)
    sine = jnp.sin(angle)
    rotation = identity.at[first, first].set(cosine).at[second, second].set(cosine)
    rotation = rotation.at[first, second].set(-sine).at[second, first].set(sine)
    return rotation


def coupling_matrix(key):
    key_rates = jax.random.fold_in(key, 21)
    key_angles = jax.random.fold_in(key, 22)
    key_signs = jax.random.fold_in(key, 23)
    rates = jax.random.uniform(key_rates, (5,), jnp.float32, 1.0, 2.0)
    keeping = jnp.exp(-rates / MESH_SPAN_EAST).astype(jnp.float32)
    magnitudes = jax.random.uniform(key_angles, (5,), jnp.float32, 0.2, 0.5)
    signs = jnp.where(jax.random.uniform(key_signs, (5,), jnp.float32) < 0.5, -1.0, 1.0)
    angles = magnitudes * signs
    planes = [(0, 1), (2, 3), (1, 2), (3, 4), (0, 4)]
    rotation = jnp.eye(5, dtype=jnp.float32)
    for position in range(5):
        first, second = planes[position]
        turned = plane_rotation(5, first, second, angles[position])
        rotation = jnp.dot(turned, rotation, precision=lax.Precision.HIGHEST)
    return keeping[:, None] * rotation / 0.1


def draw_lower_coupling(key, part):
    return coupling_matrix(jax.random.fold_in(key, 31))


def draw_upper_neighbour_block(key, part):
    return coupling_matrix(jax.random.fold_in(key, 32))


def plant(result, key, smallest, top_value):
    longest = result.shape.index(max(result.shape))
    spots = []
    for shift in (0, 1):
        where = [jax.random.randint(jax.random.fold_in(key, axis), (), 0, length) for axis, length in enumerate(result.shape)]
        where[longest] = (where[longest] + shift) % result.shape[longest]
        spots.append(tuple(where))
    return result.at[spots[0]].set(smallest).at[spots[1]].set(top_value)


def steps_of(stream_key, extent, split, low, top_value):
    level, own = 1.0, jax.random.fold_in(stream_key, 6)
    for dim, blocks in split:
        heights = jnp.exp(jax.random.uniform(jax.random.fold_in(own, dim), (blocks,), jnp.float32, low / len(split), top_value / len(split)))
        level = level * jnp.repeat(heights, extent[dim] // blocks).reshape([-1 if axis == dim else 1 for axis in range(len(extent))])
    return level


def gaussian(stream_key, shape, scale, limit, split=(), held_as=jnp.bfloat16):
    drawn = scale * jax.random.normal(stream_key, shape, jnp.float32)
    if split:
        drawn = drawn * steps_of(stream_key, shape, split, -0.22, 0.18)
    return jnp.clip(drawn, -limit, limit).astype(held_as)


def setup_inputs(seed: int = 0) -> dict:
    key_of = jax.random.split(jax.random.key(seed), 12)
    state_field = gaussian(key_of[0], (MESH_SPAN_EAST, COMP, NY, NZ), 1.0, 6.0, ((0, 16), (2, 8), (3, 2)), jnp.float32)
    source = gaussian(key_of[1], (MESH_SPAN_EAST, COMP, NY, NZ), 1.0, 6.0, ((0, 16), (2, 8), (3, 2)), jnp.float32)
    fluid_mask = plant((jax.random.randint(key_of[2], (MESH_SPAN_EAST, NY, NZ), 0, 16) < 15).astype(jnp.int32), jax.random.fold_in(key_of[2], 1), 0, 1)
    cell_kind = plant(jax.random.randint(key_of[3], (MESH_SPAN_EAST, NY, NZ), 0, 3), jax.random.fold_in(key_of[3], 1), 0, 2).astype(jnp.int32)
    boundary_side_number = plant(jax.random.randint(key_of[4], (MESH_SPAN_EAST, NY, NZ), 0, 12), jax.random.fold_in(key_of[4], 1), 0, 11).astype(jnp.int32)
    center_matrix = gaussian(key_of[5], (COMP, COMP), COMP ** -0.5, 2.5, (), jnp.float32)
    flux_jacobian_blocks = gaussian(key_of[6], (6, COMP, COMP), 0.2, 1.0, (), jnp.float32)
    wall_matrix = gaussian(key_of[7], (COMP, COMP), COMP ** -0.5, 2.5, (), jnp.float32)
    diag_inverse = draw_diag_inverse(jax.random.fold_in(key_of[11], 71), 0)
    lower_coupling = draw_lower_coupling(jax.random.fold_in(key_of[11], 71), 0)
    upper_neighbour_block = draw_upper_neighbour_block(jax.random.fold_in(key_of[11], 71), 0)
    return dict(state_field=state_field, source=source, fluid_mask=fluid_mask, cell_kind=cell_kind, boundary_side_number=boundary_side_number, center_matrix=center_matrix, flux_jacobian_blocks=flux_jacobian_blocks, wall_matrix=wall_matrix, diag_inverse=diag_inverse, lower_coupling=lower_coupling, upper_neighbour_block=upper_neighbour_block)


def const_apply(matrix, vector):
    return jnp.einsum("ab,...byz->...ayz", matrix, vector, precision=lax.Precision.HIGHEST)


def volume_operator(blocks, vector):
    return jnp.sum(blocks * vector[..., None, :, :, :], axis=-3)


def flux_residual(state_field, padded, source, fluid, cell_kind, boundary_side_number, center_matrix, flux_jacobian_blocks, wall_matrix):
    neighbours = [padded[:-2, :, 1:-1, 1:-1], padded[2:, :, 1:-1, 1:-1],
                  padded[1:-1, :, :-2, 1:-1], padded[1:-1, :, 2:, 1:-1],
                  padded[1:-1, :, 1:-1, :-2], padded[1:-1, :, 1:-1, 2:]]
    walled = const_apply(wall_matrix, state_field)
    flux = const_apply(center_matrix, state_field)
    for facing in range(6):
        at_wall = (boundary_side_number == facing)[:, None]
        flux = flux + jnp.where(at_wall, walled, const_apply(flux_jacobian_blocks[facing], neighbours[facing]))
    weight = jnp.where(cell_kind == 0, 1.0, jnp.where(cell_kind == 1, 2.0, 4.0)).astype(jnp.float32)
    return fluid[:, None] * (source - flux) * weight[:, None]


def reference(state_field, source, fluid_mask, cell_kind, boundary_side_number, center_matrix, flux_jacobian_blocks, wall_matrix, diag_inverse, lower_coupling, upper_neighbour_block):
    fluid = fluid_mask.astype(jnp.float32)
    masked = state_field * fluid[:, None]
    padded = jnp.pad(masked, ((1, 1), (0, 0), (1, 1), (1, 1)))
    residual = flux_residual(state_field, padded, source, fluid, cell_kind, boundary_side_number, center_matrix, flux_jacobian_blocks, wall_matrix)

    def forward(carry, inputs):
        blocks, term = inputs
        carry = volume_operator(blocks, term + const_apply(lower_coupling, carry))
        return carry, carry

    def backward(carry, inputs):
        blocks, value = inputs
        carry = value - volume_operator(blocks, const_apply(upper_neighbour_block, carry))
        return carry, carry

    zeroed = jnp.zeros((COMP, NY, NZ), jnp.float32)
    final, swept = lax.scan(forward, zeroed, (diag_inverse, residual))
    final, update = lax.scan(backward, zeroed, (diag_inverse, swept), reverse=True)
    return update, residual
```

```python
import functools

import jax
import jax.numpy as jnp
from jax import lax
from jax.experimental import pallas as pl
from jax.experimental.pallas import tpu as pltpu
from jax.sharding import PartitionSpec as P

MESH = pl.DeviceIdType.MESH
F32 = jnp.float32
ROWS_T = 32
ROWS_B = 56
ROWS_V = 8


def aligned(start, size):
    return pl.ds(pl.multiple_of(start, 8), size)


def total(terms):
    terms = list(terms)
    while len(terms) > 1:
        terms = [a + b for a, b in zip(terms[::2], terms[1::2])] + terms[len(terms) & ~1:]
    return terms[0]


def kernel(
    n, ny,
    state_hbm, source_hbm, fluid_hbm, kind_hbm, side_hbm, diag_hbm,
    center, jac, wall, lower, upper,
    update_hbm, residual_hbm,
    state, source, fluid, kind, side, diag,
    masked, ysend, yrecv, zrecv,
    dl, du, tf, g, sw, res, upd,
    send_t, recv_t, send_b, recv_b, send_v, recv_v, send_r, recv_r,
    in_sem, out_sem, halo_send, halo_recv, x_send, x_recv,
):
    planes, comps, rows, lanes = state.shape
    cells = comps * rows
    me = lax.axis_index("gx")
    my = lax.axis_index("gy")
    mz = lax.axis_index("gz")
    east, west = lax.rem(me + 1, n), lax.rem(me + n - 1, n)
    north, south = lax.rem(my + 1, ny), lax.rem(my + ny - 1, ny)

    loads = [
        pltpu.make_async_copy(hbm, vmem, in_sem.at[i])
        for i, (hbm, vmem) in enumerate(
            [(state_hbm, state), (fluid_hbm, fluid), (diag_hbm, diag), (source_hbm, source), (side_hbm, side), (kind_hbm, kind)]
        )
    ]
    for load in loads:
        load.start()

    barrier = pltpu.get_barrier_semaphore()
    for k in range(1, n):
        pl.semaphore_signal(barrier, inc=1, device_id={"gx": lax.rem(me + k, n)}, device_id_type=MESH)
    for other in (north, south):
        pl.semaphore_signal(barrier, inc=1, device_id={"gy": other}, device_id_type=MESH)
    pl.semaphore_signal(barrier, inc=1, device_id={"gz": 1 - mz}, device_id_type=MESH)

    loads[0].wait()
    loads[1].wait()

    def mask_plane(x, _):
        keep = fluid[x].astype(F32)
        for c in range(comps):
            masked[aligned((x + 1) * cells + c * rows, rows), :] = state[x, c] * keep
        return 0

    lax.fori_loop(0, planes, mask_plane, 0)
    ysend[0] = masked[pl.ds(cells + rows - 1, planes * comps, stride=rows), :]
    ysend[1] = masked[pl.ds(cells, planes * comps, stride=rows), :]
    pl.semaphore_wait(barrier, n + 2)

    def remote(src, dst, send_sem, recv_sem, where):
        return pltpu.make_async_remote_copy(
            src_ref=src, dst_ref=dst, send_sem=send_sem, recv_sem=recv_sem, device_id=where, device_id_type=MESH
        )

    halos = [
        remote(ysend.at[0], yrecv.at[0], halo_send.at[0], halo_recv.at[0], {"gy": north}),
        remote(ysend.at[1], yrecv.at[1], halo_send.at[1], halo_recv.at[1], {"gy": south}),
        remote(
            masked.at[pl.ds(planes * cells, cells)], masked.at[pl.ds(0, cells)],
            halo_send.at[2], halo_recv.at[2], {"gx": east},
        ),
        remote(
            masked.at[pl.ds(cells, cells)], masked.at[pl.ds((planes + 1) * cells, cells)],
            halo_send.at[3], halo_recv.at[3], {"gx": west},
        ),
        remote(masked.at[pl.ds(cells, planes * cells)], zrecv, halo_send.at[4], halo_recv.at[4], {"gz": 1 - mz}),
    ]
    for halo in halos:
        halo.start()

    loads[2].wait()

    def products(x, _):
        for a in range(comps):
            row = [diag[x, a, b] for b in range(comps)]
            for c in range(comps):
                dl[x, a, c] = total(row[b] * lower[b, c] for b in range(comps))
                du[x, a, c] = total(row[b] * upper[b, c] for b in range(comps))
        return 0

    lax.fori_loop(0, planes, products, 0)

    def columns(ref, x, half):
        return [ref[x, :, b, aligned(half * 8, 8), :] for b in range(comps)]

    def times(block, column):
        return total(block[b] * column[b][None] for b in range(comps))

    def exchange(src, dst, size, slot, k):
        peer = lax.rem(me + k, n)
        return remote(
            src.at[aligned(peer * size, size)], dst.at[aligned(me * size, size)],
            x_send.at[slot, k], x_recv.at[slot, k], {"gx": peer},
        )

    def start_all(src, dst, size, slot):
        def one(k, _):
            exchange(src, dst, size, slot, k).start()
            return 0

        lax.fori_loop(1, n, one, 0)
        dst[aligned(me * size, size), :] = src[aligned(me * size, size), :]

    def wait_all(src, dst, size, slot):
        def one(k, _):
            exchange(src, dst, size, slot, k).wait_recv()
            return 0

        lax.fori_loop(1, n, one, 0)

    def wait_sent(src, dst, size, slot):
        def one(k, _):
            exchange(src, dst, size, slot, k).wait_send()
            return 0

        lax.fori_loop(1, n, one, 0)

    def forward_maps(half, _):
        def step(x, held):
            block = columns(dl, x, half)
            held = [times(block, column) for column in held]
            for b in range(comps):
                tf[x, :, b, aligned(half * 8, 8), :] = held[b]
            return held

        first = columns(dl, 0, half)
        for b in range(comps):
            tf[0, :, b, aligned(half * 8, 8), :] = first[b]
        last = lax.fori_loop(1, planes, step, first)
        for a in range(comps):
            for b in range(comps):
                send_t[pl.ds(half * 8 * ROWS_T + a * comps + b, 8, stride=ROWS_T), :] = last[b][a]
        return 0

    for half in range(rows // 8):
        forward_maps(half, 0)
    start_all(send_t, recv_t, ROWS_T, 0)

    def backward_maps(half, _):
        def through(turn, held):
            x = planes - 2 - turn
            block = columns(du, x, half)
            return [tf[x, :, b, aligned(half * 8, 8), :] - times(block, held[b]) for b in range(comps)]

        def back(turn, held):
            x = planes - 2 - turn
            block = columns(du, x, half)
            return [-times(block, column) for column in held]

        last = lax.fori_loop(0, planes - 1, through, columns(tf, planes - 1, half))
        for a in range(comps):
            for b in range(comps):
                send_b[pl.ds(half * 8 * ROWS_B + a * comps + b, 8, stride=ROWS_B), :] = last[b][a]
        last = lax.fori_loop(0, planes - 1, back, [-column for column in columns(du, planes - 1, half)])
        for a in range(comps):
            for b in range(comps):
                send_b[pl.ds(half * 8 * ROWS_B + 25 + a * comps + b, 8, stride=ROWS_B), :] = last[b][a]
        return 0

    for half in range(rows // 8):
        backward_maps(half, 0)
    start_all(send_b, recv_b, ROWS_B, 1)

    for halo in halos:
        halo.wait_recv()
    yrecv[0] = jnp.where(my == 0, 0.0, yrecv[0])
    yrecv[1] = jnp.where(my == ny - 1, 0.0, yrecv[1])
    masked[0:cells, :] = jnp.where(me == 0, 0.0, masked[0:cells, :])
    top = pl.ds((planes + 1) * cells, cells)
    masked[top, :] = jnp.where(me == n - 1, 0.0, masked[top, :])
    for i in range(3, 6):
        loads[i].wait()

    row_id = lax.broadcasted_iota(jnp.int32, (rows, lanes), 0)
    lane_id = lax.broadcasted_iota(jnp.int32, (rows, lanes), 1)
    from_low = jnp.where(mz == 0, 0.0, 1.0).astype(F32)
    from_high = 1.0 - from_low

    def residual_planes(step, _):
        xs = (2 * step, 2 * step + 1)
        sides = [side[x] for x in xs]
        flux = [[None] * comps for _ in xs]

        def add(matrix, b, values):
            for a in range(comps):
                weight = matrix(a, b)
                for i, value in enumerate(values):
                    term = weight * value
                    flux[i][a] = term if flux[i][a] is None else flux[i][a] + term

        for b in range(comps):
            own = [state[x, b] for x in xs]
            add(lambda a, b: center[a, b], b, own)
            add(lambda a, b: wall[a, b], b, [jnp.where(s < 6, v, 0.0) for s, v in zip(sides, own)])
            here = [masked[aligned((x + 1) * cells + b * rows, rows), :] for x in xs]
            other = [zrecv[aligned(x * cells + b * rows, rows), :] for x in xs]
            neighbours = [
                [masked[aligned(x * cells + b * rows, rows), :] for x in xs],
                [masked[aligned((x + 2) * cells + b * rows, rows), :] for x in xs],
                [
                    jnp.where(row_id == 0, yrecv[0, pl.ds(x * comps + b, 1), :], pltpu.roll(v, 1, 0))
                    for x, v in zip(xs, here)
                ],
                [
                    jnp.where(row_id == rows - 1, yrecv[1, pl.ds(x * comps + b, 1), :], pltpu.roll(v, rows - 1, 0))
                    for x, v in zip(xs, here)
                ],
                [pltpu.roll(jnp.where(lane_id == lanes - 1, o * from_low, v), 1, 1) for o, v in zip(other, here)],
                [pltpu.roll(jnp.where(lane_id == 0, o * from_high, v), lanes - 1, 1) for o, v in zip(other, here)],
            ]
            for d in range(6):
                add(
                    lambda a, b: jac[d, a, b], b,
                    [jnp.where(s == d, 0.0, v) for s, v in zip(sides, neighbours[d])],
                )
        for i, x in enumerate(xs):
            flag = kind[x]
            weight = jnp.where(flag == 0, 1.0, jnp.where(flag == 1, 2.0, 4.0)) * fluid[x].astype(F32)
            out = [(source[x, a] - flux[i][a]) * weight for a in range(comps)]
            for a in range(comps):
                res[x, a] = out[a]
            for a in range(comps):
                g[x, a] = total(diag[x, a, b] * out[b] for b in range(comps))
        return 0

    lax.fori_loop(0, planes // 2, residual_planes, 0)
    res_out = pltpu.make_async_copy(res, residual_hbm, out_sem.at[0])
    res_out.start()

    def forward(x, held):
        held = [
            g[x, a] + total(dl[x, a, b] * held[b] for b in range(comps)) for a in range(comps)
        ]
        for a in range(comps):
            sw[x, a] = held[a]
        return held

    def backward(turn, held):
        x = planes - 1 - turn
        return [
            sw[x, a] - total(du[x, a, b] * held[b] for b in range(comps)) for a in range(comps)
        ]

    zeros = [jnp.zeros((rows, lanes), F32)] * comps
    held = lax.fori_loop(0, planes, forward, zeros)
    for c in range(comps):
        send_v[0, pl.ds(c, rows, stride=ROWS_V), :] = held[c]
    start_all(send_v.at[0], recv_v.at[0], ROWS_V, 2)
    held = lax.fori_loop(0, planes, backward, zeros)
    for c in range(comps):
        send_v[1, pl.ds(c, rows, stride=ROWS_V), :] = held[c]
    start_all(send_v.at[1], recv_v.at[1], ROWS_V, 3)

    def apply(ref, start, vector):
        return total(ref[pl.ds(start + b, comps, stride=comps), :] * vector[b:b + 1] for b in range(comps))

    wait_all(send_t, recv_t, ROWS_T, 0)
    wait_all(send_v.at[0], recv_v.at[0], ROWS_V, 2)
    came = jnp.zeros((comps, lanes), F32)
    forward_in = []
    for i in range(n):
        forward_in.append(came)
        send_r[0, pl.ds(i * ROWS_V, comps), :] = came
        if i < n - 1:
            came = recv_v[0, pl.ds(i * ROWS_V, comps), :] + apply(recv_t, i * ROWS_T, came)
    start_all(send_r.at[0], recv_r.at[0], ROWS_V, 4)
    wait_all(send_b, recv_b, ROWS_B, 1)
    wait_all(send_v.at[1], recv_v.at[1], ROWS_V, 3)
    came = jnp.zeros((comps, lanes), F32)
    for i in range(n - 1, -1, -1):
        send_r[1, pl.ds(i * ROWS_V, comps), :] = came
        if i > 0:
            came = (
                recv_v[1, pl.ds(i * ROWS_V, comps), :] + apply(recv_b, i * ROWS_B, forward_in[i])
                + apply(recv_b, i * ROWS_B + 25, came)
            )
    start_all(send_r.at[1], recv_r.at[1], ROWS_V, 5)

    wait_all(send_r.at[0], recv_r.at[0], ROWS_V, 4)
    held = [recv_r[0, pl.ds(c, rows, stride=ROWS_V), :] for c in range(comps)]
    lax.fori_loop(0, planes, forward, held)
    wait_all(send_r.at[1], recv_r.at[1], ROWS_V, 5)
    held = [recv_r[1, pl.ds(c, rows, stride=ROWS_V), :] for c in range(comps)]

    def finish(turn, held):
        x = planes - 1 - turn
        held = backward(turn, held)
        for a in range(comps):
            upd[x, a] = held[a]
        return held

    lax.fori_loop(0, planes, finish, held)
    upd_out = pltpu.make_async_copy(upd, update_hbm, out_sem.at[1])
    upd_out.start()
    for halo in halos:
        halo.wait_send()
    wait_sent(send_t, recv_t, ROWS_T, 0)
    wait_sent(send_b, recv_b, ROWS_B, 1)
    wait_sent(send_v.at[0], recv_v.at[0], ROWS_V, 2)
    wait_sent(send_v.at[1], recv_v.at[1], ROWS_V, 3)
    wait_sent(send_r.at[0], recv_r.at[0], ROWS_V, 4)
    wait_sent(send_r.at[1], recv_r.at[1], ROWS_V, 5)
    res_out.wait()
    upd_out.wait()


def on_device(n, ny, state_field, source, fluid_mask, cell_kind, boundary_side_number, center_matrix,
              flux_jacobian_blocks, wall_matrix, diag_inverse, lower_coupling, upper_neighbour_block):
    planes, comps, rows, lanes = state_field.shape
    assert rows == n and comps == 5 and rows % 8 == 0 and planes % 2 == 0
    cells = comps * rows
    vmem = pltpu.VMEM
    field = vmem((planes, comps, rows, lanes), F32)
    flags = vmem((planes, rows, lanes), jnp.int32)
    blocks = vmem((planes, comps, comps, rows, lanes), F32)
    hbm = pl.BlockSpec(memory_space=pl.ANY)
    smem = pl.BlockSpec(memory_space=pltpu.SMEM)
    out = jax.ShapeDtypeStruct(state_field.shape, F32)
    return pl.pallas_call(
        functools.partial(kernel, n, ny),
        out_shape=(out, out),
        in_specs=[hbm] * 6 + [smem] * 5,
        out_specs=(hbm, hbm),
        scratch_shapes=[
            field, field, flags, flags, flags, blocks,
            vmem(((planes + 2) * cells, lanes), F32),
            vmem((2, planes * comps, lanes), F32),
            vmem((2, planes * comps, lanes), F32),
            vmem((planes * cells, lanes), F32),
            blocks, blocks, blocks, field, field, field, field,
            vmem((n * ROWS_T, lanes), F32), vmem((n * ROWS_T, lanes), F32),
            vmem((n * ROWS_B, lanes), F32), vmem((n * ROWS_B, lanes), F32),
            vmem((2, n * ROWS_V, lanes), F32), vmem((2, n * ROWS_V, lanes), F32),
            vmem((2, n * ROWS_V, lanes), F32), vmem((2, n * ROWS_V, lanes), F32),
            pltpu.SemaphoreType.DMA((6,)), pltpu.SemaphoreType.DMA((2,)),
            pltpu.SemaphoreType.DMA((5,)), pltpu.SemaphoreType.DMA((5,)),
            pltpu.SemaphoreType.DMA((6, n)), pltpu.SemaphoreType.DMA((6, n)),
        ],
        compiler_params=pltpu.CompilerParams(
            collective_id=0, has_side_effects=True, vmem_limit_bytes=48 * 1024 * 1024
        ),
    )(state_field, source, fluid_mask, cell_kind, boundary_side_number, diag_inverse,
      center_matrix, flux_jacobian_blocks, wall_matrix, lower_coupling, upper_neighbour_block)


def solution(mesh):
    field = P("gx", None, "gy", "gz")
    flags = P("gx", "gy", "gz")
    return jax.shard_map(
        functools.partial(on_device, mesh.shape["gx"], mesh.shape["gy"]),
        mesh=mesh,
        in_specs=(field, field, flags, flags, flags, P(), P(), P(), P("gx", None, None, "gy", "gz"), P(), P()),
        out_specs=(field, field),
        check_vma=False,
    )
```

```python
import functools

import jax
import jax.numpy as jnp
from jax import lax
from jax.experimental import pallas as pl
from jax.experimental.pallas import tpu as pltpu
from jax.sharding import PartitionSpec as P

MESH = pl.DeviceIdType.MESH
F32 = jnp.float32
GROUP = 4
MAPS = 75
ROWS_M = 80
ROWS_V = 16


def aligned(start, size):
    return pl.ds(pl.multiple_of(start, 8), size)


def total(terms):
    terms = list(terms)
    while len(terms) > 1:
        terms = [a + b for a, b in zip(terms[::2], terms[1::2])] + terms[len(terms) & ~1:]
    return terms[0]


def times(block, column):
    return total(part * column[b][None] for b, part in enumerate(block))


def kernel(
    n, ny,
    state_hbm, source_hbm, fluid_hbm, kind_hbm, side_hbm, diag_hbm,
    center, jac, wall, lower, upper,
    update_hbm, residual_hbm,
    state, source, fluid, kind, side, diag,
    masked, ysend, yrecv, zrecv,
    dl, du, tf, g, sw, res, upd,
    send_m1, recv_m1, send_v1, recv_v1, send_r1, recv_r1, left_back,
    send_m2, recv_m2, send_v2, recv_v2, send_r2, recv_r2,
    in_sem, out_sem, halo_send, halo_recv, x_send, x_recv,
):
    planes, comps, rows, lanes = state.shape
    cells = comps * rows
    quarter = rows // GROUP
    me = lax.axis_index("gx")
    my = lax.axis_index("gy")
    mz = lax.axis_index("gz")
    spot, group = lax.rem(me, GROUP), me // GROUP
    east, west = lax.rem(me + 1, n), lax.rem(me + n - 1, n)
    north, south = lax.rem(my + 1, ny), lax.rem(my + ny - 1, ny)
    in_group = [(p, me - spot + p) for p in (lax.rem(spot + k, GROUP) for k in range(1, GROUP))]
    across = [(p, p * GROUP + spot) for p in (lax.rem(group + k, GROUP) for k in range(1, GROUP))]

    pairs = [
        (diag_hbm, diag), (state_hbm, state), (fluid_hbm, fluid), (source_hbm, source), (side_hbm, side), (kind_hbm, kind)
    ]
    loads = [pltpu.make_async_copy(hbm, vmem, in_sem.at[i]) for i, (hbm, vmem) in enumerate(pairs)]
    loads[1].start()
    loads[2].start()
    loads[0].start()

    barrier = pltpu.get_barrier_semaphore()
    for _, peer in in_group + across + [(0, east), (0, west)]:
        pl.semaphore_signal(barrier, inc=1, device_id={"gx": peer}, device_id_type=MESH)
    for other in (north, south):
        pl.semaphore_signal(barrier, inc=1, device_id={"gy": other}, device_id_type=MESH)
    pl.semaphore_signal(barrier, inc=1, device_id={"gz": 1 - mz}, device_id_type=MESH)

    loads[1].wait()
    loads[2].wait()

    def mask_plane(x, _):
        keep = fluid[aligned(x * rows, rows), :].astype(F32)
        for c in range(comps):
            masked[aligned((x + 1) * cells + c * rows, rows), :] = state[x, c] * keep
        return 0

    lax.fori_loop(0, planes, mask_plane, 0)
    ysend[0] = masked[pl.ds(cells + rows - 1, planes * comps, stride=rows), :]
    ysend[1] = masked[pl.ds(cells, planes * comps, stride=rows), :]

    loads[0].wait()
    for i in range(3, 6):
        loads[i].start()

    def products(x, _):
        for a in range(comps):
            row = [diag[x, a, b] for b in range(comps)]
            for c in range(comps):
                dl[x, a, c] = total(row[b] * lower[b, c] for b in range(comps))
                du[x, a, c] = total(row[b] * upper[b, c] for b in range(comps))
        return 0

    lax.fori_loop(0, planes, products, 0)

    def columns(ref, x, half):
        return [ref[x, :, b, aligned(half * 8, 8), :] for b in range(comps)]

    def pack(part, half, held):
        for b in range(comps):
            for a in range(comps):
                for i in range(8 // quarter):
                    send_m1[half * (8 // quarter) + i, part * 25 + b * comps + a] = (
                        held[b][a, i * quarter:(i + 1) * quarter]
                    )

    def forward_maps(half):
        def step(x, held):
            block = columns(dl, x, half)
            held = [times(block, column) for column in held]
            for b in range(comps):
                tf[x, :, b, aligned(half * 8, 8), :] = held[b]
            return held

        first = columns(dl, 0, half)
        for b in range(comps):
            tf[0, :, b, aligned(half * 8, 8), :] = first[b]
        pack(0, half, lax.fori_loop(1, planes, step, first))

    for half in range(rows // 8):
        forward_maps(half)

    def remote(src, dst, send_sem, recv_sem, where):
        return pltpu.make_async_remote_copy(
            src_ref=src, dst_ref=dst, send_sem=send_sem, recv_sem=recv_sem, device_id=where, device_id_type=MESH
        )

    halos = [
        remote(ysend.at[0], yrecv.at[0], halo_send.at[0], halo_recv.at[0], {"gy": north}),
        remote(ysend.at[1], yrecv.at[1], halo_send.at[1], halo_recv.at[1], {"gy": south}),
        remote(
            masked.at[pl.ds(planes * cells, cells)], masked.at[pl.ds(0, cells)],
            halo_send.at[2], halo_recv.at[2], {"gx": east},
        ),
        remote(
            masked.at[pl.ds(cells, cells)], masked.at[pl.ds((planes + 1) * cells, cells)],
            halo_send.at[3], halo_recv.at[3], {"gx": west},
        ),
        remote(masked.at[pl.ds(cells, planes * cells)], zrecv, halo_send.at[4], halo_recv.at[4], {"gz": 1 - mz}),
    ]

    def swap_in_group(src, dst, slot, part):
        return [
            remote(
                src.at[p, part], dst.at[spot, part], x_send.at[slot, k], x_recv.at[slot, k], {"gx": peer}
            )
            for k, (p, peer) in enumerate(in_group)
        ]

    def swap_across(src, dst, size, slot):
        return [
            remote(
                src.at[aligned(p * size, size)], dst.at[aligned(group * size, size)],
                x_send.at[slot, k], x_recv.at[slot, k], {"gx": peer},
            )
            for k, (p, peer) in enumerate(across)
        ]

    maps_a = swap_in_group(send_m1, recv_m1, 0, pl.ds(0, 25))
    maps_b = swap_in_group(send_m1, recv_m1, 1, pl.ds(25, 50))
    maps_2 = swap_across(send_m2, recv_m2, ROWS_M, 2)
    ends_1 = swap_in_group(send_v1, recv_v1, 3, pl.ds(0, 2 * comps))
    ends_2 = swap_across(send_v2, recv_v2, ROWS_V, 4)
    back_2 = swap_across(send_r2, recv_r2, ROWS_V, 5)
    back_1 = swap_in_group(send_r1, recv_r1, 6, pl.ds(0, 2 * comps))

    def start(copies):
        for copy in copies:
            copy.start()

    def arrive(copies):
        for copy in copies:
            copy.wait_recv()

    def keep_own(src, dst, size):
        dst[aligned(group * size, size), :] = src[aligned(group * size, size), :]

    pl.semaphore_wait(barrier, 2 * (GROUP - 1) + 5)
    start(halos)
    start(maps_a)

    def backward_maps(half):
        def through(turn, held):
            x = planes - 2 - turn
            block = columns(du, x, half)
            return [tf[x, :, b, aligned(half * 8, 8), :] - times(block, held[b]) for b in range(comps)]

        def back(turn, held):
            x = planes - 2 - turn
            block = columns(du, x, half)
            return [-times(block, column) for column in held]

        pack(1, half, lax.fori_loop(0, planes - 1, through, columns(tf, planes - 1, half)))
        pack(2, half, lax.fori_loop(0, planes - 1, back, [-column for column in columns(du, planes - 1, half)]))

    for half in range(rows // 8):
        backward_maps(half)
    start(maps_b)
    recv_m1[spot] = send_m1[spot]

    arrive(halos[2:])
    masked[0:cells, :] = jnp.where(me == 0, 0.0, masked[0:cells, :])
    top = pl.ds((planes + 1) * cells, cells)
    masked[top, :] = jnp.where(me == n - 1, 0.0, masked[top, :])
    for i in range(3, 6):
        loads[i].wait()

    row_id = lax.broadcasted_iota(jnp.int32, (rows, lanes), 0)
    lane_id = lax.broadcasted_iota(jnp.int32, (rows, lanes), 1)
    from_low = jnp.where(mz == 0, 0.0, 1.0).astype(F32)
    from_high = 1.0 - from_low

    def weights(flag, wet):
        return jnp.where(flag == 0, 1.0, jnp.where(flag == 1, 2.0, 4.0)) * wet.astype(F32)

    def residual_planes(step, _):
        xs = (2 * step, 2 * step + 1)
        sides = [side[aligned(x * rows, rows), :] for x in xs]
        flux = [[None] * comps for _ in xs]

        def add(matrix, b, values):
            for a in range(comps):
                weight = matrix(a, b)
                for i, value in enumerate(values):
                    term = weight * value
                    flux[i][a] = term if flux[i][a] is None else flux[i][a] + term

        for b in range(comps):
            own = [state[x, b] for x in xs]
            add(lambda a, b: center[a, b], b, own)
            add(lambda a, b: wall[a, b], b, [jnp.where(s < 6, v, 0.0) for s, v in zip(sides, own)])
            here = [masked[aligned((x + 1) * cells + b * rows, rows), :] for x in xs]
            other = [zrecv[aligned(x * cells + b * rows, rows), :] for x in xs]
            neighbours = [
                [masked[aligned(x * cells + b * rows, rows), :] for x in xs],
                [masked[aligned((x + 2) * cells + b * rows, rows), :] for x in xs],
                [pltpu.roll(v, 1, 0) for v in here],
                [pltpu.roll(v, rows - 1, 0) for v in here],
                [pltpu.roll(jnp.where(lane_id == lanes - 1, o * from_low, v), 1, 1) for o, v in zip(other, here)],
                [pltpu.roll(jnp.where(lane_id == 0, o * from_high, v), lanes - 1, 1) for o, v in zip(other, here)],
            ]
            edge = [None, None, 0, rows - 1, None, None]
            for d in range(6):
                closed = [s == d for s in sides]
                if edge[d] is not None:
                    closed = [jnp.logical_or(c, row_id == edge[d]) for c in closed]
                add(lambda a, b: jac[a, d, b], b, [jnp.where(c, 0.0, v) for c, v in zip(closed, neighbours[d])])
        for i, x in enumerate(xs):
            weight = weights(kind[aligned(x * rows, rows), :], fluid[aligned(x * rows, rows), :])
            for a in range(comps):
                res[aligned(x * cells + a * rows, rows), :] = (source[x, a] - flux[i][a]) * weight
        return 0

    lax.fori_loop(0, planes // 2, residual_planes, 0)

    arrive(halos[:2])
    for i, (d, row) in enumerate(((2, 0), (3, rows - 1))):
        edge_rows = pl.ds(row, planes, stride=rows)
        is_open = jnp.logical_and(side[edge_rows, :] != d, my != (0, ny - 1)[i])
        weight = jnp.where(is_open, weights(kind[edge_rows, :], fluid[edge_rows, :]), 0.0)
        beyond = [yrecv[i, pl.ds(b, planes, stride=comps), :] for b in range(comps)]
        for a in range(comps):
            at = pl.ds(a * rows + row, planes, stride=cells)
            res[at, :] = res[at, :] - weight * total(jac[a, d, b] * beyond[b] for b in range(comps))
    res_out = pltpu.make_async_copy(res, residual_hbm, out_sem.at[0])
    res_out.start()

    def first_forward(x, held):
        terms = [res[aligned(x * cells + b * rows, rows), :] for b in range(comps)]
        for a in range(comps):
            g[x, a] = total(diag[x, a, b] * terms[b] for b in range(comps))
        return forward(x, held)

    def forward(x, held):
        held = [
            g[x, a] + total(dl[x, a, b] * held[b] for b in range(comps)) for a in range(comps)
        ]
        for a in range(comps):
            sw[x, a] = held[a]
        return held

    def backward(turn, held):
        x = planes - 1 - turn
        return [
            sw[x, a] - total(du[x, a, b] * held[b] for b in range(comps)) for a in range(comps)
        ]

    zeros = [jnp.zeros((rows, lanes), F32)] * comps
    east_end = lax.fori_loop(0, planes, first_forward, zeros)
    west_end = lax.fori_loop(0, planes, backward, zeros)
    for c, value in enumerate(list(east_end) + list(west_end)):
        for i in range(GROUP):
            send_v1[i, c] = value[i * quarter:(i + 1) * quarter]
    start(ends_1)
    recv_v1[spot] = send_v1[spot]

    def held_map(d, part):
        return [recv_m1[d, pl.ds(part * 25 + b * comps, comps)] for b in range(comps)]

    arrive(maps_a)
    arrive(maps_b)
    ahead, through, behind = [held_map(0, part) for part in range(3)]
    for d in range(1, GROUP):
        for b in range(comps):
            left_back[d, pl.ds(b * comps, comps)] = behind[b]
        own_through = held_map(d, 1)
        turned = [times(own_through, column) for column in ahead]
        through = [through[b] + times(behind, turned[b]) for b in range(comps)]
        own_ahead = held_map(d, 0)
        ahead = [times(own_ahead, column) for column in ahead]
        behind = [times(behind, column) for column in held_map(d, 2)]
    for part, columns_of in enumerate((ahead, through, behind)):
        for b in range(comps):
            for a in range(comps):
                send_m2[pl.ds(part * 25 + a * comps + b, GROUP, stride=ROWS_M), :] = columns_of[b][a]
    start(maps_2)
    keep_own(send_m2, recv_m2, ROWS_M)

    arrive(ends_1)
    forward_end = recv_v1[0, pl.ds(0, comps)]
    backward_end = recv_v1[0, pl.ds(comps, comps)]
    for d in range(1, GROUP):
        turned = recv_v1[d, pl.ds(comps, comps)] + times(held_map(d, 1), forward_end)
        left = [left_back[d, pl.ds(b * comps, comps)] for b in range(comps)]
        backward_end = backward_end + times(left, turned)
        forward_end = recv_v1[d, pl.ds(0, comps)] + times(held_map(d, 0), forward_end)
    for c in range(comps):
        send_v2[pl.ds(c, GROUP, stride=ROWS_V), :] = forward_end[c]
        send_v2[pl.ds(8 + c, GROUP, stride=ROWS_V), :] = backward_end[c]
    start(ends_2)
    keep_own(send_v2, recv_v2, ROWS_V)

    def apply(start_row, vector):
        return total(
            recv_m2[pl.ds(start_row + b, comps, stride=comps), :] * vector[b:b + 1] for b in range(comps)
        )

    arrive(maps_2)
    arrive(ends_2)
    came = jnp.zeros((comps, lanes), F32)
    forward_in = []
    for i in range(GROUP):
        forward_in.append(came)
        send_r2[pl.ds(i * ROWS_V, comps), :] = came
        if i < GROUP - 1:
            came = recv_v2[pl.ds(i * ROWS_V, comps), :] + apply(i * ROWS_M, came)
    came = jnp.zeros((comps, lanes), F32)
    for i in range(GROUP - 1, -1, -1):
        send_r2[pl.ds(i * ROWS_V + 8, comps), :] = came
        if i > 0:
            came = (
                recv_v2[pl.ds(i * ROWS_V + 8, comps), :] + apply(i * ROWS_M + 25, forward_in[i])
                + apply(i * ROWS_M + 50, came)
            )
    start(back_2)
    keep_own(send_r2, recv_r2, ROWS_V)

    arrive(back_2)
    came = jnp.stack([recv_r2[pl.ds(c, GROUP, stride=ROWS_V), :] for c in range(comps)])
    forward_in = []
    for d in range(GROUP):
        forward_in.append(came)
        send_r1[d, pl.ds(0, comps)] = came
        if d < GROUP - 1:
            came = recv_v1[d, pl.ds(0, comps)] + times(held_map(d, 0), came)
    came = jnp.stack([recv_r2[pl.ds(8 + c, GROUP, stride=ROWS_V), :] for c in range(comps)])
    for d in range(GROUP - 1, -1, -1):
        send_r1[d, pl.ds(comps, comps)] = came
        if d > 0:
            came = (
                recv_v1[d, pl.ds(comps, comps)] + times(held_map(d, 1), forward_in[d]) + times(held_map(d, 2), came)
            )
    start(back_1)
    recv_r1[spot] = send_r1[spot]

    arrive(back_1)
    came = [
        jnp.concatenate([recv_r1[i, c] for i in range(GROUP)], axis=0) for c in range(2 * comps)
    ]
    lax.fori_loop(0, planes, forward, came[:comps])

    def finish(turn, held):
        x = planes - 1 - turn
        held = backward(turn, held)
        for a in range(comps):
            upd[x, a] = held[a]
        return held

    lax.fori_loop(0, planes, finish, came[comps:])
    upd_out = pltpu.make_async_copy(upd, update_hbm, out_sem.at[1])
    upd_out.start()
    for copy in halos + maps_a + maps_b + maps_2 + ends_1 + ends_2 + back_2 + back_1:
        copy.wait_send()
    res_out.wait()
    upd_out.wait()


def on_device(n, ny, state_field, source, fluid_mask, cell_kind, boundary_side_number, center_matrix,
              flux_jacobian_blocks, wall_matrix, diag_inverse, lower_coupling, upper_neighbour_block):
    planes, comps, rows, lanes = state_field.shape
    assert n == GROUP * GROUP and rows == n and comps == 5 and planes % 2 == 0
    cells = comps * rows
    quarter = rows // GROUP
    vmem = pltpu.VMEM
    field = vmem((planes, comps, rows, lanes), F32)
    flags = vmem((planes * rows, lanes), jnp.int32)
    blocks = vmem((planes, comps, comps, rows, lanes), F32)
    maps = vmem((GROUP, MAPS, quarter, lanes), F32)
    ends = vmem((GROUP, 2 * comps, quarter, lanes), F32)
    maps_across = vmem((GROUP * ROWS_M, lanes), F32)
    ends_across = vmem((GROUP * ROWS_V, lanes), F32)
    hbm = pl.BlockSpec(memory_space=pl.ANY)
    smem = pl.BlockSpec(memory_space=pltpu.SMEM)
    update, residual = pl.pallas_call(
        functools.partial(kernel, n, ny),
        out_shape=(
            jax.ShapeDtypeStruct(state_field.shape, F32),
            jax.ShapeDtypeStruct((planes * cells, lanes), F32),
        ),
        in_specs=[hbm] * 6 + [smem] * 5,
        out_specs=(hbm, hbm),
        scratch_shapes=[
            field, field, flags, flags, flags, blocks,
            vmem(((planes + 2) * cells, lanes), F32),
            vmem((2, planes * comps, lanes), F32),
            vmem((2, planes * comps, lanes), F32),
            vmem((planes * cells, lanes), F32),
            blocks, blocks, blocks, field, field, vmem((planes * cells, lanes), F32), field,
            maps, maps, ends, ends, ends, ends, vmem((GROUP, 25, quarter, lanes), F32),
            maps_across, maps_across, ends_across, ends_across, ends_across, ends_across,
            pltpu.SemaphoreType.DMA((6,)), pltpu.SemaphoreType.DMA((2,)),
            pltpu.SemaphoreType.DMA((5,)), pltpu.SemaphoreType.DMA((5,)),
            pltpu.SemaphoreType.DMA((7, GROUP - 1)), pltpu.SemaphoreType.DMA((7, GROUP - 1)),
        ],
        compiler_params=pltpu.CompilerParams(
            collective_id=0, has_side_effects=True, vmem_limit_bytes=63 * 1024 * 1024
        ),
    )(
        state_field, source, *(a.reshape(planes * rows, lanes) for a in (fluid_mask, cell_kind, boundary_side_number)),
        diag_inverse, center_matrix, jnp.transpose(flux_jacobian_blocks, (1, 0, 2)), wall_matrix,
        lower_coupling, upper_neighbour_block,
    )
    return update, residual.reshape(state_field.shape)


def solution(mesh):
    field = P("gx", None, "gy", "gz")
    flags = P("gx", "gy", "gz")
    return jax.shard_map(
        functools.partial(on_device, mesh.shape["gx"], mesh.shape["gy"]),
        mesh=mesh,
        in_specs=(field, field, flags, flags, flags, P(), P(), P(), P("gx", None, None, "gy", "gz"), P(), P()),
        out_specs=(field, field),
        check_vma=False,
    )
```

```python
import functools

import jax
import jax.numpy as jnp
from jax import lax
from jax.experimental import pallas as pl
from jax.experimental.pallas import tpu as pltpu
from jax.sharding import PartitionSpec as P

MESH = pl.DeviceIdType.MESH
F32 = jnp.float32
GROUP = 4
MAPS = 75
ROWS_M = 80
ROWS_V = 16


def aligned(start, size):
    return pl.ds(pl.multiple_of(start, 8), size)


def total(terms):
    terms = list(terms)
    while len(terms) > 1:
        terms = [a + b for a, b in zip(terms[::2], terms[1::2])] + terms[len(terms) & ~1:]
    return terms[0]


def times(block, column):
    return total(part * column[b][None] for b, part in enumerate(block))


def kernel(
    n, ny,
    state_hbm, source_hbm, fluid_hbm, kind_hbm, side_hbm, diag_hbm,
    center, jac, wall, lower, upper,
    upd, res,
    state, source, fluid, kind, side, diag,
    masked, ysend, yrecv, zrecv,
    dl, du, tf, g, sw,
    send_m1, recv_m1, send_v1, recv_v1, send_r1, recv_r1, left_back,
    send_m2, recv_m2, send_v2, recv_v2, send_r2, recv_r2,
    in_sem, halo_send, halo_recv, x_send, x_recv,
):
    planes, comps, rows, lanes = state.shape
    cells = comps * rows
    quarter = rows // GROUP
    me = lax.axis_index("gx")
    my = lax.axis_index("gy")
    mz = lax.axis_index("gz")
    spot, group = lax.rem(me, GROUP), me // GROUP
    east, west = lax.rem(me + 1, n), lax.rem(me + n - 1, n)
    north, south = lax.rem(my + 1, ny), lax.rem(my + ny - 1, ny)
    in_group = [(p, me - spot + p) for p in (lax.rem(spot + k, GROUP) for k in range(1, GROUP))]
    across = [(p, p * GROUP + spot) for p in (lax.rem(group + k, GROUP) for k in range(1, GROUP))]

    pairs = [
        (diag_hbm, diag), (state_hbm, state), (fluid_hbm, fluid), (source_hbm, source), (side_hbm, side), (kind_hbm, kind)
    ]
    loads = [pltpu.make_async_copy(hbm, vmem, in_sem.at[i]) for i, (hbm, vmem) in enumerate(pairs)]
    loads[1].start()
    loads[2].start()
    loads[0].start()

    barrier = pltpu.get_barrier_semaphore()
    for _, peer in in_group + across + [(0, east), (0, west)]:
        pl.semaphore_signal(barrier, inc=1, device_id={"gx": peer}, device_id_type=MESH)
    for other in (north, south):
        pl.semaphore_signal(barrier, inc=1, device_id={"gy": other}, device_id_type=MESH)
    pl.semaphore_signal(barrier, inc=1, device_id={"gz": 1 - mz}, device_id_type=MESH)

    loads[1].wait()
    loads[2].wait()

    def mask_plane(x, _):
        keep = fluid[aligned(x * rows, rows), :].astype(F32)
        for c in range(comps):
            masked[aligned((x + 1) * cells + c * rows, rows), :] = state[x, c] * keep
        return 0

    lax.fori_loop(0, planes, mask_plane, 0)
    ysend[0] = masked[pl.ds(cells + rows - 1, planes * comps, stride=rows), :]
    ysend[1] = masked[pl.ds(cells, planes * comps, stride=rows), :]

    loads[0].wait()
    for i in range(3, 6):
        loads[i].start()

    def products(x, _):
        for a in range(comps):
            row = [diag[x, a, b] for b in range(comps)]
            for c in range(comps):
                dl[x, a, c] = total(row[b] * lower[b, c] for b in range(comps))
                du[x, a, c] = total(row[b] * upper[b, c] for b in range(comps))
        return 0

    lax.fori_loop(0, planes, products, 0)

    def columns(ref, x, half):
        return [ref[x, :, b, aligned(half * 8, 8), :] for b in range(comps)]

    def pack(part, half, held):
        for b in range(comps):
            for a in range(comps):
                for i in range(8 // quarter):
                    send_m1[half * (8 // quarter) + i, part * 25 + b * comps + a] = (
                        held[b][a, i * quarter:(i + 1) * quarter]
                    )

    def forward_maps(half):
        def step(x, held):
            block = columns(dl, x, half)
            held = [times(block, column) for column in held]
            for b in range(comps):
                tf[x, :, b, aligned(half * 8, 8), :] = held[b]
            return held

        first = columns(dl, 0, half)
        for b in range(comps):
            tf[0, :, b, aligned(half * 8, 8), :] = first[b]
        pack(0, half, lax.fori_loop(1, planes, step, first))

    for half in range(rows // 8):
        forward_maps(half)

    def remote(src, dst, send_sem, recv_sem, where):
        return pltpu.make_async_remote_copy(
            src_ref=src, dst_ref=dst, send_sem=send_sem, recv_sem=recv_sem, device_id=where, device_id_type=MESH
        )

    halos = [
        remote(ysend.at[0], yrecv.at[0], halo_send.at[0], halo_recv.at[0], {"gy": north}),
        remote(ysend.at[1], yrecv.at[1], halo_send.at[1], halo_recv.at[1], {"gy": south}),
        remote(
            masked.at[pl.ds(planes * cells, cells)], masked.at[pl.ds(0, cells)],
            halo_send.at[2], halo_recv.at[2], {"gx": east},
        ),
        remote(
            masked.at[pl.ds(cells, cells)], masked.at[pl.ds((planes + 1) * cells, cells)],
            halo_send.at[3], halo_recv.at[3], {"gx": west},
        ),
        remote(masked.at[pl.ds(cells, planes * cells)], zrecv, halo_send.at[4], halo_recv.at[4], {"gz": 1 - mz}),
    ]

    def swap_in_group(src, dst, slot, part):
        return [
            remote(
                src.at[p, part], dst.at[spot, part], x_send.at[slot, k], x_recv.at[slot, k], {"gx": peer}
            )
            for k, (p, peer) in enumerate(in_group)
        ]

    def swap_across(src, dst, size, slot):
        return [
            remote(
                src.at[aligned(p * size, size)], dst.at[aligned(group * size, size)],
                x_send.at[slot, k], x_recv.at[slot, k], {"gx": peer},
            )
            for k, (p, peer) in enumerate(across)
        ]

    maps_a = swap_in_group(send_m1, recv_m1, 0, pl.ds(0, 25))
    maps_b = swap_in_group(send_m1, recv_m1, 1, pl.ds(25, 50))
    maps_2 = swap_across(send_m2, recv_m2, ROWS_M, 2)
    ends_1 = swap_in_group(send_v1, recv_v1, 3, pl.ds(0, 2 * comps))
    ends_2 = swap_across(send_v2, recv_v2, ROWS_V, 4)
    back_2 = swap_across(send_r2, recv_r2, ROWS_V, 5)
    back_1 = swap_in_group(send_r1, recv_r1, 6, pl.ds(0, 2 * comps))

    def start(copies):
        for copy in copies:
            copy.start()

    def arrive(copies):
        for copy in copies:
            copy.wait_recv()

    def keep_own(src, dst, size):
        dst[aligned(group * size, size), :] = src[aligned(group * size, size), :]

    pl.semaphore_wait(barrier, 2 * (GROUP - 1) + 5)
    start(halos)
    start(maps_a)

    def backward_maps(half):
        def through(turn, held):
            x = planes - 2 - turn
            block = columns(du, x, half)
            return [tf[x, :, b, aligned(half * 8, 8), :] - times(block, held[b]) for b in range(comps)]

        def back(turn, held):
            x = planes - 2 - turn
            block = columns(du, x, half)
            return [-times(block, column) for column in held]

        pack(1, half, lax.fori_loop(0, planes - 1, through, columns(tf, planes - 1, half)))
        pack(2, half, lax.fori_loop(0, planes - 1, back, [-column for column in columns(du, planes - 1, half)]))

    for half in range(rows // 8):
        backward_maps(half)
    start(maps_b)
    recv_m1[spot] = send_m1[spot]

    arrive(halos[2:])
    masked[0:cells, :] = jnp.where(me == 0, 0.0, masked[0:cells, :])
    top = pl.ds((planes + 1) * cells, cells)
    masked[top, :] = jnp.where(me == n - 1, 0.0, masked[top, :])
    for i in range(3, 6):
        loads[i].wait()

    row_id = lax.broadcasted_iota(jnp.int32, (rows, lanes), 0)
    lane_id = lax.broadcasted_iota(jnp.int32, (rows, lanes), 1)
    from_low = jnp.where(mz == 0, 0.0, 1.0).astype(F32)
    from_high = 1.0 - from_low

    def weights(flag, wet):
        return jnp.where(flag == 0, 1.0, jnp.where(flag == 1, 2.0, 4.0)) * wet.astype(F32)

    def residual_planes(step, _):
        xs = (2 * step, 2 * step + 1)
        sides = [side[aligned(x * rows, rows), :] for x in xs]
        flux = [[None] * comps for _ in xs]

        def add(matrix, b, values):
            for a in range(comps):
                weight = matrix(a, b)
                for i, value in enumerate(values):
                    term = weight * value
                    flux[i][a] = term if flux[i][a] is None else flux[i][a] + term

        for b in range(comps):
            own = [state[x, b] for x in xs]
            add(lambda a, b: center[a, b], b, own)
            add(lambda a, b: wall[a, b], b, [jnp.where(s < 6, v, 0.0) for s, v in zip(sides, own)])
            here = [masked[aligned((x + 1) * cells + b * rows, rows), :] for x in xs]
            other = [zrecv[aligned(x * cells + b * rows, rows), :] for x in xs]
            neighbours = [
                [masked[aligned(x * cells + b * rows, rows), :] for x in xs],
                [masked[aligned((x + 2) * cells + b * rows, rows), :] for x in xs],
                [pltpu.roll(v, 1, 0) for v in here],
                [pltpu.roll(v, rows - 1, 0) for v in here],
                [pltpu.roll(jnp.where(lane_id == lanes - 1, o * from_low, v), 1, 1) for o, v in zip(other, here)],
                [pltpu.roll(jnp.where(lane_id == 0, o * from_high, v), lanes - 1, 1) for o, v in zip(other, here)],
            ]
            edge = [None, None, 0, rows - 1, None, None]
            for d in range(6):
                closed = [s == d for s in sides]
                if edge[d] is not None:
                    closed = [jnp.logical_or(c, row_id == edge[d]) for c in closed]
                add(lambda a, b: jac[a, d, b], b, [jnp.where(c, 0.0, v) for c, v in zip(closed, neighbours[d])])
        for i, x in enumerate(xs):
            weight = weights(kind[aligned(x * rows, rows), :], fluid[aligned(x * rows, rows), :])
            for a in range(comps):
                res[aligned(x * cells + a * rows, rows), :] = (source[x, a] - flux[i][a]) * weight
        return 0

    lax.fori_loop(0, planes // 2, residual_planes, 0)

    arrive(halos[:2])
    for i, (d, row) in enumerate(((2, 0), (3, rows - 1))):
        edge_rows = pl.ds(row, planes, stride=rows)
        is_open = jnp.logical_and(side[edge_rows, :] != d, my != (0, ny - 1)[i])
        weight = jnp.where(is_open, weights(kind[edge_rows, :], fluid[edge_rows, :]), 0.0)
        beyond = [yrecv[i, pl.ds(b, planes, stride=comps), :] for b in range(comps)]
        for a in range(comps):
            at = pl.ds(a * rows + row, planes, stride=cells)
            res[at, :] = res[at, :] - weight * total(jac[a, d, b] * beyond[b] for b in range(comps))

    def first_forward(x, held):
        terms = [res[aligned(x * cells + b * rows, rows), :] for b in range(comps)]
        for a in range(comps):
            g[x, a] = total(diag[x, a, b] * terms[b] for b in range(comps))
        return forward(x, held)

    def forward(x, held):
        held = [
            g[x, a] + total(dl[x, a, b] * held[b] for b in range(comps)) for a in range(comps)
        ]
        for a in range(comps):
            sw[x, a] = held[a]
        return held

    def backward(turn, held):
        x = planes - 1 - turn
        return [
            sw[x, a] - total(du[x, a, b] * held[b] for b in range(comps)) for a in range(comps)
        ]

    zeros = [jnp.zeros((rows, lanes), F32)] * comps
    east_end = lax.fori_loop(0, planes, first_forward, zeros)
    west_end = lax.fori_loop(0, planes, backward, zeros)
    for c, value in enumerate(list(east_end) + list(west_end)):
        for i in range(GROUP):
            send_v1[i, c] = value[i * quarter:(i + 1) * quarter]
    start(ends_1)
    recv_v1[spot] = send_v1[spot]

    def held_map(d, part):
        return [recv_m1[d, pl.ds(part * 25 + b * comps, comps)] for b in range(comps)]

    arrive(maps_a)
    arrive(maps_b)
    ahead, through, behind = [held_map(0, part) for part in range(3)]
    for d in range(1, GROUP):
        for b in range(comps):
            left_back[d, pl.ds(b * comps, comps)] = behind[b]
        own_through = held_map(d, 1)
        turned = [times(own_through, column) for column in ahead]
        through = [through[b] + times(behind, turned[b]) for b in range(comps)]
        own_ahead = held_map(d, 0)
        ahead = [times(own_ahead, column) for column in ahead]
        behind = [times(behind, column) for column in held_map(d, 2)]
    for part, columns_of in enumerate((ahead, through, behind)):
        for b in range(comps):
            for a in range(comps):
                send_m2[pl.ds(part * 25 + a * comps + b, GROUP, stride=ROWS_M), :] = columns_of[b][a]
    start(maps_2)
    keep_own(send_m2, recv_m2, ROWS_M)

    arrive(ends_1)
    forward_end = recv_v1[0, pl.ds(0, comps)]
    backward_end = recv_v1[0, pl.ds(comps, comps)]
    for d in range(1, GROUP):
        turned = recv_v1[d, pl.ds(comps, comps)] + times(held_map(d, 1), forward_end)
        left = [left_back[d, pl.ds(b * comps, comps)] for b in range(comps)]
        backward_end = backward_end + times(left, turned)
        forward_end = recv_v1[d, pl.ds(0, comps)] + times(held_map(d, 0), forward_end)
    for c in range(comps):
        send_v2[pl.ds(c, GROUP, stride=ROWS_V), :] = forward_end[c]
        send_v2[pl.ds(8 + c, GROUP, stride=ROWS_V), :] = backward_end[c]
    start(ends_2)
    keep_own(send_v2, recv_v2, ROWS_V)

    def apply(start_row, vector):
        return total(
            recv_m2[pl.ds(start_row + b, comps, stride=comps), :] * vector[b:b + 1] for b in range(comps)
        )

    arrive(maps_2)
    arrive(ends_2)
    came = jnp.zeros((comps, lanes), F32)
    forward_in = []
    for i in range(GROUP):
        forward_in.append(came)
        send_r2[pl.ds(i * ROWS_V, comps), :] = came
        if i < GROUP - 1:
            came = recv_v2[pl.ds(i * ROWS_V, comps), :] + apply(i * ROWS_M, came)
    came = jnp.zeros((comps, lanes), F32)
    for i in range(GROUP - 1, -1, -1):
        send_r2[pl.ds(i * ROWS_V + 8, comps), :] = came
        if i > 0:
            came = (
                recv_v2[pl.ds(i * ROWS_V + 8, comps), :] + apply(i * ROWS_M + 25, forward_in[i])
                + apply(i * ROWS_M + 50, came)
            )
    start(back_2)
    keep_own(send_r2, recv_r2, ROWS_V)

    arrive(back_2)
    came = jnp.stack([recv_r2[pl.ds(c, GROUP, stride=ROWS_V), :] for c in range(comps)])
    forward_in = []
    for d in range(GROUP):
        forward_in.append(came)
        send_r1[d, pl.ds(0, comps)] = came
        if d < GROUP - 1:
            came = recv_v1[d, pl.ds(0, comps)] + times(held_map(d, 0), came)
    came = jnp.stack([recv_r2[pl.ds(8 + c, GROUP, stride=ROWS_V), :] for c in range(comps)])
    for d in range(GROUP - 1, -1, -1):
        send_r1[d, pl.ds(comps, comps)] = came
        if d > 0:
            came = (
                recv_v1[d, pl.ds(comps, comps)] + times(held_map(d, 1), forward_in[d]) + times(held_map(d, 2), came)
            )
    start(back_1)
    recv_r1[spot] = send_r1[spot]

    arrive(back_1)
    came = [
        jnp.concatenate([recv_r1[i, c] for i in range(GROUP)], axis=0) for c in range(2 * comps)
    ]
    lax.fori_loop(0, planes, forward, came[:comps])

    def finish(turn, held):
        x = planes - 1 - turn
        held = backward(turn, held)
        for a in range(comps):
            upd[x, a] = held[a]
        return held

    lax.fori_loop(0, planes, finish, came[comps:])
    for copy in halos + maps_a + maps_b + maps_2 + ends_1 + ends_2 + back_2 + back_1:
        copy.wait_send()


def on_device(n, ny, state_field, source, fluid_mask, cell_kind, boundary_side_number, center_matrix,
              flux_jacobian_blocks, wall_matrix, diag_inverse, lower_coupling, upper_neighbour_block):
    planes, comps, rows, lanes = state_field.shape
    assert n == GROUP * GROUP and rows == n and comps == 5 and planes % 2 == 0
    cells = comps * rows
    quarter = rows // GROUP
    vmem = pltpu.VMEM
    field = vmem((planes, comps, rows, lanes), F32)
    flags = vmem((planes * rows, lanes), jnp.int32)
    blocks = vmem((planes, comps, comps, rows, lanes), F32)
    maps = vmem((GROUP, MAPS, quarter, lanes), F32)
    ends = vmem((GROUP, 2 * comps, quarter, lanes), F32)
    maps_across = vmem((GROUP * ROWS_M, lanes), F32)
    ends_across = vmem((GROUP * ROWS_V, lanes), F32)
    hbm = pl.BlockSpec(memory_space=pltpu.HBM)
    smem = pl.BlockSpec(memory_space=pltpu.SMEM)
    update, residual = pl.pallas_call(
        functools.partial(kernel, n, ny),
        out_shape=(
            pltpu.VMEM(state_field.shape, F32),
            pltpu.VMEM((planes * cells, lanes), F32),
        ),
        in_specs=[hbm] * 6 + [smem] * 5,
        out_specs=(pl.BlockSpec(memory_space=pltpu.VMEM),) * 2,
        scratch_shapes=[
            field, field, flags, flags, flags, blocks,
            vmem(((planes + 2) * cells, lanes), F32),
            vmem((2, planes * comps, lanes), F32),
            vmem((2, planes * comps, lanes), F32),
            vmem((planes * cells, lanes), F32),
            blocks, blocks, blocks, field, field,
            maps, maps, ends, ends, ends, ends, vmem((GROUP, 25, quarter, lanes), F32),
            maps_across, maps_across, ends_across, ends_across, ends_across, ends_across,
            pltpu.SemaphoreType.DMA((6,)),
            pltpu.SemaphoreType.DMA((5,)), pltpu.SemaphoreType.DMA((5,)),
            pltpu.SemaphoreType.DMA((7, GROUP - 1)), pltpu.SemaphoreType.DMA((7, GROUP - 1)),
        ],
        compiler_params=pltpu.CompilerParams(
            collective_id=0, has_side_effects=True, vmem_limit_bytes=61 * 1024 * 1024
        ),
    )(
        state_field, source, *(a.reshape(planes * rows, lanes) for a in (fluid_mask, cell_kind, boundary_side_number)),
        diag_inverse, center_matrix, jnp.transpose(flux_jacobian_blocks, (1, 0, 2)), wall_matrix,
        lower_coupling, upper_neighbour_block,
    )
    return write(update, residual.reshape(state_field.shape))


def write_kernel(update, residual, update_out, residual_out, sems):
    copies = [
        pltpu.make_async_copy(update, update_out, sems.at[0]),
        pltpu.make_async_copy(residual, residual_out, sems.at[1]),
    ]
    for copy in copies:
        copy.start()
    for copy in copies:
        copy.wait()


def write(update, residual):
    return pl.pallas_call(
        write_kernel,
        out_shape=(jax.ShapeDtypeStruct(update.shape, F32), jax.ShapeDtypeStruct(residual.shape, F32)),
        in_specs=[pl.BlockSpec(memory_space=pltpu.VMEM)] * 2,
        out_specs=(pl.BlockSpec(memory_space=pltpu.HBM),) * 2,
        scratch_shapes=[pltpu.SemaphoreType.DMA((2,))],
        compiler_params=pltpu.CompilerParams(vmem_limit_bytes=1024 * 1024),
    )(update, residual)


def solution(mesh):
    field = P("gx", None, "gy", "gz")
    flags = P("gx", "gy", "gz")
    return jax.shard_map(
        functools.partial(on_device, mesh.shape["gx"], mesh.shape["gy"]),
        mesh=mesh,
        in_specs=(field, field, flags, flags, flags, P(), P(), P(), P("gx", None, None, "gy", "gz"), P(), P()),
        out_specs=(field, field),
        check_vma=False,
    )
```

```python
import functools

import jax
import jax.numpy as jnp
from jax import lax
from jax.experimental import pallas as pl
from jax.experimental.pallas import tpu as pltpu
from jax.sharding import PartitionSpec as P

MESH = pl.DeviceIdType.MESH
F32 = jnp.float32
GROUP = 4
MAPS = 75
ROWS_M = 80
ROWS_V = 16


def aligned(start, size):
    return pl.ds(pl.multiple_of(start, 8), size)


def total(terms):
    terms = list(terms)
    while len(terms) > 1:
        terms = [a + b for a, b in zip(terms[::2], terms[1::2])] + terms[len(terms) & ~1:]
    return terms[0]


def times(block, column):
    return total(part * column[b][None] for b, part in enumerate(block))


def kernel(
    n, ny,
    state_hbm, source_hbm, fluid_hbm, kind_hbm, side_hbm, diag_hbm,
    center_hbm, jac_hbm, wall_hbm, lower_hbm, upper_hbm,
    upd, res,
    center, jac, wall, lower, upper,
    state, source, fluid, kind, side, diag,
    masked, ysend, yrecv, zrecv,
    dl, du, tf, g, sw,
    send_m1, recv_m1, send_v1, recv_v1, send_r1, recv_r1, left_back,
    send_m2, recv_m2, send_v2, recv_v2, send_r2, recv_r2,
    in_sem, halo_send, halo_recv, x_send, x_recv,
):
    planes, comps, rows, lanes = state.shape
    cells = comps * rows
    quarter = rows // GROUP
    me = lax.axis_index("gx")
    my = lax.axis_index("gy")
    mz = lax.axis_index("gz")
    spot, group = lax.rem(me, GROUP), me // GROUP
    east, west = lax.rem(me + 1, n), lax.rem(me + n - 1, n)
    north, south = lax.rem(my + 1, ny), lax.rem(my + ny - 1, ny)
    in_group = [(p, me - spot + p) for p in (lax.rem(spot + k, GROUP) for k in range(1, GROUP))]
    across = [(p, p * GROUP + spot) for p in (lax.rem(group + k, GROUP) for k in range(1, GROUP))]

    pairs = [
        (diag_hbm, diag), (state_hbm, state), (fluid_hbm, fluid), (source_hbm, source), (side_hbm, side), (kind_hbm, kind),
        (lower_hbm, lower), (upper_hbm, upper), (center_hbm, center), (wall_hbm, wall), (jac_hbm, jac),
    ]
    loads = [pltpu.make_async_copy(hbm, vmem, in_sem.at[i]) for i, (hbm, vmem) in enumerate(pairs)]
    barrier = pltpu.get_barrier_semaphore()
    for other in (north, south):
        pl.semaphore_signal(barrier, inc=1, device_id={"gy": other}, device_id_type=MESH)
    for _, peer in [(0, east), (0, west)] + across + in_group:
        pl.semaphore_signal(barrier, inc=1, device_id={"gx": peer}, device_id_type=MESH)
    pl.semaphore_signal(barrier, inc=1, device_id={"gz": 1 - mz}, device_id_type=MESH)
    for i in (1, 2, 6, 7, 0, 8, 9, 10):
        loads[i].start()

    loads[1].wait()
    loads[2].wait()

    def mask_plane(x, _):
        keep = fluid[aligned(x * rows, rows), :].astype(F32)
        for c in range(comps):
            masked[aligned((x + 1) * cells + c * rows, rows), :] = state[x, c] * keep
        return 0

    lax.fori_loop(0, planes, mask_plane, 0)
    ysend[0] = masked[pl.ds(cells + rows - 1, planes * comps, stride=rows), :]
    ysend[1] = masked[pl.ds(cells, planes * comps, stride=rows), :]

    for i in (6, 7, 0):
        loads[i].wait()
    for i in range(3, 6):
        loads[i].start()

    def products(x, _):
        for a in range(comps):
            row = [diag[x, a, b] for b in range(comps)]
            for c in range(comps):
                dl[x, a, c] = total(row[b] * lower[b, c] for b in range(comps))
                du[x, a, c] = total(row[b] * upper[b, c] for b in range(comps))
        return 0

    lax.fori_loop(0, planes, products, 0)

    def columns(ref, x, half):
        return [ref[x, :, b, aligned(half * 8, 8), :] for b in range(comps)]

    def pack(part, half, held):
        for b in range(comps):
            for a in range(comps):
                for i in range(8 // quarter):
                    send_m1[half * (8 // quarter) + i, part * 25 + b * comps + a] = (
                        held[b][a, i * quarter:(i + 1) * quarter]
                    )

    def forward_maps(half):
        def step(x, held):
            block = columns(dl, x, half)
            held = [times(block, column) for column in held]
            for b in range(comps):
                tf[x, :, b, aligned(half * 8, 8), :] = held[b]
            return held

        first = columns(dl, 0, half)
        for b in range(comps):
            tf[0, :, b, aligned(half * 8, 8), :] = first[b]
        pack(0, half, lax.fori_loop(1, planes, step, first))

    for half in range(rows // 8):
        forward_maps(half)

    def remote(src, dst, send_sem, recv_sem, where):
        return pltpu.make_async_remote_copy(
            src_ref=src, dst_ref=dst, send_sem=send_sem, recv_sem=recv_sem, device_id=where, device_id_type=MESH
        )

    halos = [
        remote(ysend.at[0], yrecv.at[0], halo_send.at[0], halo_recv.at[0], {"gy": north}),
        remote(ysend.at[1], yrecv.at[1], halo_send.at[1], halo_recv.at[1], {"gy": south}),
        remote(
            masked.at[pl.ds(planes * cells, cells)], masked.at[pl.ds(0, cells)],
            halo_send.at[2], halo_recv.at[2], {"gx": east},
        ),
        remote(
            masked.at[pl.ds(cells, cells)], masked.at[pl.ds((planes + 1) * cells, cells)],
            halo_send.at[3], halo_recv.at[3], {"gx": west},
        ),
        remote(masked.at[pl.ds(cells, planes * cells)], zrecv, halo_send.at[4], halo_recv.at[4], {"gz": 1 - mz}),
    ]

    def swap_in_group(src, dst, slot, part):
        return [
            remote(
                src.at[p, part], dst.at[spot, part], x_send.at[slot, k], x_recv.at[slot, k], {"gx": peer}
            )
            for k, (p, peer) in enumerate(in_group)
        ]

    def swap_across(src, dst, size, slot):
        return [
            remote(
                src.at[aligned(p * size, size)], dst.at[aligned(group * size, size)],
                x_send.at[slot, k], x_recv.at[slot, k], {"gx": peer},
            )
            for k, (p, peer) in enumerate(across)
        ]

    maps_a = swap_in_group(send_m1, recv_m1, 0, pl.ds(0, 25))
    maps_b = swap_in_group(send_m1, recv_m1, 1, pl.ds(25, 50))
    maps_2 = swap_across(send_m2, recv_m2, ROWS_M, 2)
    ends_1 = swap_in_group(send_v1, recv_v1, 3, pl.ds(0, 2 * comps))
    ends_2 = swap_across(send_v2, recv_v2, ROWS_V, 4)
    back_2 = swap_across(send_r2, recv_r2, ROWS_V, 5)
    back_1 = swap_in_group(send_r1, recv_r1, 6, pl.ds(0, 2 * comps))

    def start(copies):
        for copy in copies:
            copy.start()

    def arrive(copies):
        for copy in copies:
            copy.wait_recv()

    def keep_own(src, dst, size):
        dst[aligned(group * size, size), :] = src[aligned(group * size, size), :]

    pl.semaphore_wait(barrier, 2 * (GROUP - 1) + 5)
    start(halos)
    start(maps_a)

    def backward_maps(half):
        def through(turn, held):
            x = planes - 2 - turn
            block = columns(du, x, half)
            return [tf[x, :, b, aligned(half * 8, 8), :] - times(block, held[b]) for b in range(comps)]

        def back(turn, held):
            x = planes - 2 - turn
            block = columns(du, x, half)
            return [-times(block, column) for column in held]

        pack(1, half, lax.fori_loop(0, planes - 1, through, columns(tf, planes - 1, half)))
        pack(2, half, lax.fori_loop(0, planes - 1, back, [-column for column in columns(du, planes - 1, half)]))

    for half in range(rows // 8):
        backward_maps(half)
    start(maps_b)
    recv_m1[spot] = send_m1[spot]

    arrive(halos[2:])
    masked[0:cells, :] = jnp.where(me == 0, 0.0, masked[0:cells, :])
    top = pl.ds((planes + 1) * cells, cells)
    masked[top, :] = jnp.where(me == n - 1, 0.0, masked[top, :])
    for i in (3, 4, 5, 8, 9, 10):
        loads[i].wait()

    row_id = lax.broadcasted_iota(jnp.int32, (rows, lanes), 0)
    lane_id = lax.broadcasted_iota(jnp.int32, (rows, lanes), 1)
    from_low = jnp.where(mz == 0, 0.0, 1.0).astype(F32)
    from_high = 1.0 - from_low

    def weights(flag, wet):
        return jnp.where(flag == 0, 1.0, jnp.where(flag == 1, 2.0, 4.0)) * wet.astype(F32)

    def residual_planes(step, _):
        xs = (2 * step, 2 * step + 1)
        sides = [side[aligned(x * rows, rows), :] for x in xs]
        flux = [[None] * comps for _ in xs]

        def add(matrix, b, values):
            for a in range(comps):
                weight = matrix(a, b)
                for i, value in enumerate(values):
                    term = weight * value
                    flux[i][a] = term if flux[i][a] is None else flux[i][a] + term

        for b in range(comps):
            own = [state[x, b] for x in xs]
            add(lambda a, b: center[a, b], b, own)
            add(lambda a, b: wall[a, b], b, [jnp.where(s < 6, v, 0.0) for s, v in zip(sides, own)])
            here = [masked[aligned((x + 1) * cells + b * rows, rows), :] for x in xs]
            other = [zrecv[aligned(x * cells + b * rows, rows), :] for x in xs]
            neighbours = [
                [masked[aligned(x * cells + b * rows, rows), :] for x in xs],
                [masked[aligned((x + 2) * cells + b * rows, rows), :] for x in xs],
                [pltpu.roll(v, 1, 0) for v in here],
                [pltpu.roll(v, rows - 1, 0) for v in here],
                [pltpu.roll(jnp.where(lane_id == lanes - 1, o * from_low, v), 1, 1) for o, v in zip(other, here)],
                [pltpu.roll(jnp.where(lane_id == 0, o * from_high, v), lanes - 1, 1) for o, v in zip(other, here)],
            ]
            edge = [None, None, 0, rows - 1, None, None]
            for d in range(6):
                closed = [s == d for s in sides]
                if edge[d] is not None:
                    closed = [jnp.logical_or(c, row_id == edge[d]) for c in closed]
                add(lambda a, b: jac[a, d, b], b, [jnp.where(c, 0.0, v) for c, v in zip(closed, neighbours[d])])
        for i, x in enumerate(xs):
            weight = weights(kind[aligned(x * rows, rows), :], fluid[aligned(x * rows, rows), :])
            for a in range(comps):
                res[aligned(x * cells + a * rows, rows), :] = (source[x, a] - flux[i][a]) * weight
        return 0

    lax.fori_loop(0, planes // 2, residual_planes, 0)

    arrive(halos[:2])
    for i, (d, row) in enumerate(((2, 0), (3, rows - 1))):
        edge_rows = pl.ds(row, planes, stride=rows)
        is_open = jnp.logical_and(side[edge_rows, :] != d, my != (0, ny - 1)[i])
        weight = jnp.where(is_open, weights(kind[edge_rows, :], fluid[edge_rows, :]), 0.0)
        beyond = [yrecv[i, pl.ds(b, planes, stride=comps), :] for b in range(comps)]
        for a in range(comps):
            at = pl.ds(a * rows + row, planes, stride=cells)
            res[at, :] = res[at, :] - weight * total(jac[a, d, b] * beyond[b] for b in range(comps))

    def first_forward(x, held):
        terms = [res[aligned(x * cells + b * rows, rows), :] for b in range(comps)]
        for a in range(comps):
            g[x, a] = total(diag[x, a, b] * terms[b] for b in range(comps))
        return forward(x, held)

    def forward(x, held):
        held = [
            g[x, a] + total(dl[x, a, b] * held[b] for b in range(comps)) for a in range(comps)
        ]
        for a in range(comps):
            sw[x, a] = held[a]
        return held

    def backward(turn, held):
        x = planes - 1 - turn
        return [
            sw[x, a] - total(du[x, a, b] * held[b] for b in range(comps)) for a in range(comps)
        ]

    zeros = [jnp.zeros((rows, lanes), F32)] * comps
    east_end = lax.fori_loop(0, planes, first_forward, zeros)
    west_end = lax.fori_loop(0, planes, backward, zeros)
    for c, value in enumerate(list(east_end) + list(west_end)):
        for i in range(GROUP):
            send_v1[i, c] = value[i * quarter:(i + 1) * quarter]
    start(ends_1)
    recv_v1[spot] = send_v1[spot]

    def held_map(d, part):
        return [recv_m1[d, pl.ds(part * 25 + b * comps, comps)] for b in range(comps)]

    arrive(maps_a)
    arrive(maps_b)
    ahead, through, behind = [held_map(0, part) for part in range(3)]
    for d in range(1, GROUP):
        for b in range(comps):
            left_back[d, pl.ds(b * comps, comps)] = behind[b]
        own_through = held_map(d, 1)
        turned = [times(own_through, column) for column in ahead]
        through = [through[b] + times(behind, turned[b]) for b in range(comps)]
        own_ahead = held_map(d, 0)
        ahead = [times(own_ahead, column) for column in ahead]
        behind = [times(behind, column) for column in held_map(d, 2)]
    for part, columns_of in enumerate((ahead, through, behind)):
        for b in range(comps):
            for a in range(comps):
                send_m2[pl.ds(part * 25 + a * comps + b, GROUP, stride=ROWS_M), :] = columns_of[b][a]
    start(maps_2)
    keep_own(send_m2, recv_m2, ROWS_M)

    arrive(ends_1)
    forward_end = recv_v1[0, pl.ds(0, comps)]
    backward_end = recv_v1[0, pl.ds(comps, comps)]
    for d in range(1, GROUP):
        turned = recv_v1[d, pl.ds(comps, comps)] + times(held_map(d, 1), forward_end)
        left = [left_back[d, pl.ds(b * comps, comps)] for b in range(comps)]
        backward_end = backward_end + times(left, turned)
        forward_end = recv_v1[d, pl.ds(0, comps)] + times(held_map(d, 0), forward_end)
    for c in range(comps):
        send_v2[pl.ds(c, GROUP, stride=ROWS_V), :] = forward_end[c]
        send_v2[pl.ds(8 + c, GROUP, stride=ROWS_V), :] = backward_end[c]
    start(ends_2)
    keep_own(send_v2, recv_v2, ROWS_V)

    def apply(start_row, vector):
        return total(
            recv_m2[pl.ds(start_row + b, comps, stride=comps), :] * vector[b:b + 1] for b in range(comps)
        )

    arrive(maps_2)
    arrive(ends_2)
    came = jnp.zeros((comps, lanes), F32)
    forward_in = []
    for i in range(GROUP):
        forward_in.append(came)
        send_r2[pl.ds(i * ROWS_V, comps), :] = came
        if i < GROUP - 1:
            came = recv_v2[pl.ds(i * ROWS_V, comps), :] + apply(i * ROWS_M, came)
    came = jnp.zeros((comps, lanes), F32)
    for i in range(GROUP - 1, -1, -1):
        send_r2[pl.ds(i * ROWS_V + 8, comps), :] = came
        if i > 0:
            came = (
                recv_v2[pl.ds(i * ROWS_V + 8, comps), :] + apply(i * ROWS_M + 25, forward_in[i])
                + apply(i * ROWS_M + 50, came)
            )
    start(back_2)
    keep_own(send_r2, recv_r2, ROWS_V)

    arrive(back_2)
    came = jnp.stack([recv_r2[pl.ds(c, GROUP, stride=ROWS_V), :] for c in range(comps)])
    forward_in = []
    for d in range(GROUP):
        forward_in.append(came)
        send_r1[d, pl.ds(0, comps)] = came
        if d < GROUP - 1:
            came = recv_v1[d, pl.ds(0, comps)] + times(held_map(d, 0), came)
    came = jnp.stack([recv_r2[pl.ds(8 + c, GROUP, stride=ROWS_V), :] for c in range(comps)])
    for d in range(GROUP - 1, -1, -1):
        send_r1[d, pl.ds(comps, comps)] = came
        if d > 0:
            came = (
                recv_v1[d, pl.ds(comps, comps)] + times(held_map(d, 1), forward_in[d]) + times(held_map(d, 2), came)
            )
    start(back_1)
    recv_r1[spot] = send_r1[spot]

    arrive(back_1)
    came = [
        jnp.concatenate([recv_r1[i, c] for i in range(GROUP)], axis=0) for c in range(2 * comps)
    ]
    lax.fori_loop(0, planes, forward, came[:comps])

    def finish(turn, held):
        x = planes - 1 - turn
        held = backward(turn, held)
        for a in range(comps):
            upd[x, a] = held[a]
        return held

    lax.fori_loop(0, planes, finish, came[comps:])
    for copy in halos + maps_a + maps_b + maps_2 + ends_1 + ends_2 + back_2 + back_1:
        copy.wait_send()


def on_device(n, ny, state_field, source, fluid_mask, cell_kind, boundary_side_number, center_matrix,
              flux_jacobian_blocks, wall_matrix, diag_inverse, lower_coupling, upper_neighbour_block):
    planes, comps, rows, lanes = state_field.shape
    assert n == GROUP * GROUP and rows == n and comps == 5 and planes % 2 == 0
    cells = comps * rows
    quarter = rows // GROUP
    vmem = pltpu.VMEM
    field = vmem((planes, comps, rows, lanes), F32)
    flags = vmem((planes * rows, lanes), jnp.int32)
    blocks = vmem((planes, comps, comps, rows, lanes), F32)
    maps = vmem((GROUP, MAPS, quarter, lanes), F32)
    ends = vmem((GROUP, 2 * comps, quarter, lanes), F32)
    maps_across = vmem((GROUP * ROWS_M, lanes), F32)
    ends_across = vmem((GROUP * ROWS_V, lanes), F32)
    hbm = pl.BlockSpec(memory_space=pltpu.HBM)
    matrix = pltpu.SMEM((comps, comps), F32)
    update, residual = pl.pallas_call(
        functools.partial(kernel, n, ny),
        out_shape=(
            pltpu.VMEM(state_field.shape, F32),
            pltpu.VMEM((planes * cells, lanes), F32),
        ),
        in_specs=[hbm] * 11,
        out_specs=(pl.BlockSpec(memory_space=pltpu.VMEM),) * 2,
        scratch_shapes=[
            matrix, pltpu.SMEM((comps, 6, comps), F32), matrix, matrix, matrix,
            field, field, flags, flags, flags, blocks,
            vmem(((planes + 2) * cells, lanes), F32),
            vmem((2, planes * comps, lanes), F32),
            vmem((2, planes * comps, lanes), F32),
            vmem((planes * cells, lanes), F32),
            blocks, blocks, blocks, field, field,
            maps, maps, ends, ends, ends, ends, vmem((GROUP, 25, quarter, lanes), F32),
            maps_across, maps_across, ends_across, ends_across, ends_across, ends_across,
            pltpu.SemaphoreType.DMA((11,)),
            pltpu.SemaphoreType.DMA((5,)), pltpu.SemaphoreType.DMA((5,)),
            pltpu.SemaphoreType.DMA((7, GROUP - 1)), pltpu.SemaphoreType.DMA((7, GROUP - 1)),
        ],
        compiler_params=pltpu.CompilerParams(
            collective_id=0, has_side_effects=True, vmem_limit_bytes=61 * 1024 * 1024
        ),
    )(
        state_field, source, *(a.reshape(planes * rows, lanes) for a in (fluid_mask, cell_kind, boundary_side_number)),
        diag_inverse, center_matrix, jnp.transpose(flux_jacobian_blocks, (1, 0, 2)), wall_matrix,
        lower_coupling, upper_neighbour_block,
    )
    return write(update, residual.reshape(state_field.shape))


def write_kernel(update, residual, update_out, residual_out, sems):
    copies = [
        pltpu.make_async_copy(update, update_out, sems.at[0]),
        pltpu.make_async_copy(residual, residual_out, sems.at[1]),
    ]
    for copy in copies:
        copy.start()
    for copy in copies:
        copy.wait()


def write(update, residual):
    return pl.pallas_call(
        write_kernel,
        out_shape=(jax.ShapeDtypeStruct(update.shape, F32), jax.ShapeDtypeStruct(residual.shape, F32)),
        in_specs=[pl.BlockSpec(memory_space=pltpu.VMEM)] * 2,
        out_specs=(pl.BlockSpec(memory_space=pltpu.HBM),) * 2,
        scratch_shapes=[pltpu.SemaphoreType.DMA((2,))],
        compiler_params=pltpu.CompilerParams(vmem_limit_bytes=1024 * 1024),
    )(update, residual)


def solution(mesh):
    field = P("gx", None, "gy", "gz")
    flags = P("gx", "gy", "gz")
    return jax.shard_map(
        functools.partial(on_device, mesh.shape["gx"], mesh.shape["gy"]),
        mesh=mesh,
        in_specs=(field, field, flags, flags, flags, P(), P(), P(), P("gx", None, None, "gy", "gz"), P(), P()),
        out_specs=(field, field),
        check_vma=False,
    )
```

```python
import functools

import jax
import jax.numpy as jnp
from jax import lax
from jax.experimental import pallas as pl
from jax.experimental.pallas import tpu as pltpu
from jax.sharding import PartitionSpec as P

MESH = pl.DeviceIdType.MESH
F32 = jnp.float32
GROUP = 4
MAPS = 75
ROWS_M = 80
ROWS_V = 16


def aligned(start, size):
    return pl.ds(pl.multiple_of(start, 8), size)


def total(terms):
    terms = list(terms)
    while len(terms) > 1:
        terms = [a + b for a, b in zip(terms[::2], terms[1::2])] + terms[len(terms) & ~1:]
    return terms[0]


def times(block, column):
    return total(part * column[b][None] for b, part in enumerate(block))


def kernel(
    n, ny,
    state_hbm, source_hbm, fluid_hbm, kind_hbm, side_hbm, diag_hbm,
    center_hbm, jac_hbm, wall_hbm, lower_hbm, upper_hbm,
    upd, res,
    center, jac, wall, lower, upper,
    state, source, fluid, kind, side, diag,
    masked, ysend, yrecv, zrecv,
    dl, du, tf, g, sw,
    send_m1, recv_m1, send_v1, recv_v1, send_r1, recv_r1, send_mr, recv_mr,
    send_m2, recv_m2, send_v2, recv_v2, send_r2, recv_r2,
    in_sem, halo_send, halo_recv, x_send, x_recv, line_send, line_recv,
):
    planes, comps, rows, lanes = state.shape
    cells = comps * rows
    quarter = rows // GROUP
    me = lax.axis_index("gx")
    my = lax.axis_index("gy")
    mz = lax.axis_index("gz")
    spot, group = lax.rem(me, GROUP), me // GROUP
    east, west = lax.rem(me + 1, n), lax.rem(me + n - 1, n)
    north, south = lax.rem(my + 1, ny), lax.rem(my + ny - 1, ny)
    in_group = [(p, me - spot + p) for p in (lax.rem(spot + k, GROUP) for k in range(1, GROUP))]
    line = [lax.rem(me + k, n) for k in range(1, n)]
    across = [(p, p * GROUP + spot) for p in (lax.rem(group + k, GROUP) for k in range(1, GROUP))]

    pairs = [
        (diag_hbm, diag), (state_hbm, state), (fluid_hbm, fluid), (source_hbm, source), (side_hbm, side), (kind_hbm, kind),
        (lower_hbm, lower), (upper_hbm, upper), (center_hbm, center), (wall_hbm, wall), (jac_hbm, jac),
    ]
    loads = [pltpu.make_async_copy(hbm, vmem, in_sem.at[i]) for i, (hbm, vmem) in enumerate(pairs)]
    barrier = pltpu.get_barrier_semaphore()
    for other in (north, south):
        pl.semaphore_signal(barrier, inc=1, device_id={"gy": other}, device_id_type=MESH)
    for peer in line:
        pl.semaphore_signal(barrier, inc=1, device_id={"gx": peer}, device_id_type=MESH)
    pl.semaphore_signal(barrier, inc=1, device_id={"gz": 1 - mz}, device_id_type=MESH)
    for i in (1, 2, 6, 7, 0, 8, 9, 10):
        loads[i].start()

    loads[1].wait()
    loads[2].wait()

    def mask_plane(x, _):
        keep = fluid[aligned(x * rows, rows), :].astype(F32)
        for c in range(comps):
            masked[aligned((x + 1) * cells + c * rows, rows), :] = state[x, c] * keep
        return 0

    lax.fori_loop(0, planes, mask_plane, 0)
    ysend[0] = masked[pl.ds(cells + rows - 1, planes * comps, stride=rows), :]
    ysend[1] = masked[pl.ds(cells, planes * comps, stride=rows), :]

    for i in (6, 7, 0):
        loads[i].wait()
    for i in range(3, 6):
        loads[i].start()

    def products(x, _):
        for a in range(comps):
            row = [diag[x, a, b] for b in range(comps)]
            for c in range(comps):
                dl[x, a, c] = total(row[b] * lower[b, c] for b in range(comps))
                du[x, a, c] = total(row[b] * upper[b, c] for b in range(comps))
        return 0

    lax.fori_loop(0, planes, products, 0)

    def columns(ref, x, half):
        return [ref[x, :, b, aligned(half * 8, 8), :] for b in range(comps)]

    def pack(part, half, held):
        for b in range(comps):
            for a in range(comps):
                for i in range(8 // quarter):
                    send_m1[half * (8 // quarter) + i, part * 25 + b * comps + a] = (
                        held[b][a, i * quarter:(i + 1) * quarter]
                    )

    def forward_maps(half):
        def step(x, held):
            block = columns(dl, x, half)
            held = [times(block, column) for column in held]
            for b in range(comps):
                tf[x, :, b, aligned(half * 8, 8), :] = held[b]
            return held

        first = columns(dl, 0, half)
        for b in range(comps):
            tf[0, :, b, aligned(half * 8, 8), :] = first[b]
        pack(0, half, lax.fori_loop(1, planes, step, first))

    for half in range(rows // 8):
        forward_maps(half)

    def remote(src, dst, send_sem, recv_sem, where):
        return pltpu.make_async_remote_copy(
            src_ref=src, dst_ref=dst, send_sem=send_sem, recv_sem=recv_sem, device_id=where, device_id_type=MESH
        )

    halos = [
        remote(ysend.at[0], yrecv.at[0], halo_send.at[0], halo_recv.at[0], {"gy": north}),
        remote(ysend.at[1], yrecv.at[1], halo_send.at[1], halo_recv.at[1], {"gy": south}),
        remote(
            masked.at[pl.ds(planes * cells, cells)], masked.at[pl.ds(0, cells)],
            halo_send.at[2], halo_recv.at[2], {"gx": east},
        ),
        remote(
            masked.at[pl.ds(cells, cells)], masked.at[pl.ds((planes + 1) * cells, cells)],
            halo_send.at[3], halo_recv.at[3], {"gx": west},
        ),
        remote(masked.at[pl.ds(cells, planes * cells)], zrecv, halo_send.at[4], halo_recv.at[4], {"gz": 1 - mz}),
    ]

    def swap_in_group(src, dst, slot, part):
        return [
            remote(
                src.at[p, part], dst.at[spot, part], x_send.at[slot, k], x_recv.at[slot, k], {"gx": peer}
            )
            for k, (p, peer) in enumerate(in_group)
        ]

    def swap_across(src, dst, size, slot):
        return [
            remote(
                src.at[aligned(p * size, size)], dst.at[aligned(group * size, size)],
                x_send.at[slot, k], x_recv.at[slot, k], {"gx": peer},
            )
            for k, (p, peer) in enumerate(across)
        ]

    maps_a = swap_in_group(send_m1, recv_m1, 0, pl.ds(0, 25))
    maps_b = swap_in_group(send_m1, recv_m1, 1, pl.ds(25, 50))
    maps_2 = swap_across(send_m2, recv_m2, ROWS_M, 2)
    ends_1 = swap_in_group(send_v1, recv_v1, 3, pl.ds(0, 2 * comps))
    ends_2 = swap_across(send_v2, recv_v2, ROWS_V, 4)
    maps_p = swap_in_group(send_mr, recv_mr, 5, pl.ds(0, 25))
    maps_q = swap_in_group(send_mr, recv_mr, 7, pl.ds(25, 50))
    mine = spot * GROUP + group
    back_2 = [
        remote(
            send_r2.at[aligned(peer // GROUP * ROWS_V, ROWS_V)], recv_r2.at[aligned(mine * ROWS_V, ROWS_V)],
            line_send.at[k], line_recv.at[k], {"gx": peer},
        )
        for k, peer in enumerate(line)
    ]
    back_1 = swap_in_group(send_r1, recv_r1, 6, pl.ds(0, 2 * comps))

    def start(copies):
        for copy in copies:
            copy.start()

    def start_but(copies, skipped):
        for (p, _), copy in zip(in_group, copies):
            pl.when(p != skipped)(copy.start)

    def sent_but(copies, skipped):
        for (p, _), copy in zip(in_group, copies):
            pl.when(p != skipped)(copy.wait_send)

    def arrive_but(copies, skipped):
        for copy in copies:
            pl.when(spot != skipped)(copy.wait_recv)

    def arrive(copies):
        for copy in copies:
            copy.wait_recv()

    def keep_own(src, dst, size):
        dst[aligned(group * size, size), :] = src[aligned(group * size, size), :]

    pl.semaphore_wait(barrier, n + 2)
    start(halos)
    start(maps_a)

    def backward_maps(half):
        def through(turn, held):
            x = planes - 2 - turn
            block = columns(du, x, half)
            return [tf[x, :, b, aligned(half * 8, 8), :] - times(block, held[b]) for b in range(comps)]

        def back(turn, held):
            x = planes - 2 - turn
            block = columns(du, x, half)
            return [-times(block, column) for column in held]

        pack(1, half, lax.fori_loop(0, planes - 1, through, columns(tf, planes - 1, half)))
        pack(2, half, lax.fori_loop(0, planes - 1, back, [-column for column in columns(du, planes - 1, half)]))

    for half in range(rows // 8):
        backward_maps(half)
    start(maps_b)
    recv_m1[spot] = send_m1[spot]

    arrive(halos[2:])
    masked[0:cells, :] = jnp.where(me == 0, 0.0, masked[0:cells, :])
    top = pl.ds((planes + 1) * cells, cells)
    masked[top, :] = jnp.where(me == n - 1, 0.0, masked[top, :])
    for i in (3, 4, 5, 8, 9, 10):
        loads[i].wait()

    row_id = lax.broadcasted_iota(jnp.int32, (rows, lanes), 0)
    lane_id = lax.broadcasted_iota(jnp.int32, (rows, lanes), 1)
    from_low = jnp.where(mz == 0, 0.0, 1.0).astype(F32)
    from_high = 1.0 - from_low

    def weights(flag, wet):
        return jnp.where(flag == 0, 1.0, jnp.where(flag == 1, 2.0, 4.0)) * wet.astype(F32)

    def residual_planes(step, _):
        xs = (2 * step, 2 * step + 1)
        sides = [side[aligned(x * rows, rows), :] for x in xs]
        flux = [[None] * comps for _ in xs]

        def add(matrix, b, values):
            for a in range(comps):
                weight = matrix(a, b)
                for i, value in enumerate(values):
                    term = weight * value
                    flux[i][a] = term if flux[i][a] is None else flux[i][a] + term

        for b in range(comps):
            own = [state[x, b] for x in xs]
            add(lambda a, b: center[a, b], b, own)
            add(lambda a, b: wall[a, b], b, [jnp.where(s < 6, v, 0.0) for s, v in zip(sides, own)])
            here = [masked[aligned((x + 1) * cells + b * rows, rows), :] for x in xs]
            other = [zrecv[aligned(x * cells + b * rows, rows), :] for x in xs]
            neighbours = [
                [masked[aligned(x * cells + b * rows, rows), :] for x in xs],
                [masked[aligned((x + 2) * cells + b * rows, rows), :] for x in xs],
                [pltpu.roll(v, 1, 0) for v in here],
                [pltpu.roll(v, rows - 1, 0) for v in here],
                [pltpu.roll(jnp.where(lane_id == lanes - 1, o * from_low, v), 1, 1) for o, v in zip(other, here)],
                [pltpu.roll(jnp.where(lane_id == 0, o * from_high, v), lanes - 1, 1) for o, v in zip(other, here)],
            ]
            edge = [None, None, 0, rows - 1, None, None]
            for d in range(6):
                closed = [s == d for s in sides]
                if edge[d] is not None:
                    closed = [jnp.logical_or(c, row_id == edge[d]) for c in closed]
                add(lambda a, b: jac[a, d, b], b, [jnp.where(c, 0.0, v) for c, v in zip(closed, neighbours[d])])
        for i, x in enumerate(xs):
            weight = weights(kind[aligned(x * rows, rows), :], fluid[aligned(x * rows, rows), :])
            for a in range(comps):
                res[aligned(x * cells + a * rows, rows), :] = (source[x, a] - flux[i][a]) * weight
        return 0

    lax.fori_loop(0, planes // 2, residual_planes, 0)

    arrive(halos[:2])
    for i, (d, row) in enumerate(((2, 0), (3, rows - 1))):
        edge_rows = pl.ds(row, planes, stride=rows)
        is_open = jnp.logical_and(side[edge_rows, :] != d, my != (0, ny - 1)[i])
        weight = jnp.where(is_open, weights(kind[edge_rows, :], fluid[edge_rows, :]), 0.0)
        beyond = [yrecv[i, pl.ds(b, planes, stride=comps), :] for b in range(comps)]
        for a in range(comps):
            at = pl.ds(a * rows + row, planes, stride=cells)
            res[at, :] = res[at, :] - weight * total(jac[a, d, b] * beyond[b] for b in range(comps))

    def first_forward(x, held):
        terms = [res[aligned(x * cells + b * rows, rows), :] for b in range(comps)]
        for a in range(comps):
            g[x, a] = total(diag[x, a, b] * terms[b] for b in range(comps))
        return forward(x, held)

    def forward(x, held):
        held = [
            g[x, a] + total(dl[x, a, b] * held[b] for b in range(comps)) for a in range(comps)
        ]
        for a in range(comps):
            sw[x, a] = held[a]
        return held

    def backward(turn, held):
        x = planes - 1 - turn
        return [
            sw[x, a] - total(du[x, a, b] * held[b] for b in range(comps)) for a in range(comps)
        ]

    zeros = [jnp.zeros((rows, lanes), F32)] * comps
    east_end = lax.fori_loop(0, planes, first_forward, zeros)
    west_end = lax.fori_loop(0, planes, backward, zeros)
    for c, value in enumerate(list(east_end) + list(west_end)):
        for i in range(GROUP):
            send_v1[i, c] = value[i * quarter:(i + 1) * quarter]
    start(ends_1)
    recv_v1[spot] = send_v1[spot]

    def held_map(d, part):
        return [recv_m1[d, pl.ds(part * 25 + b * comps, comps)] for b in range(comps)]

    ones = jnp.ones((quarter, lanes), F32)
    same = [jnp.stack([ones if a == b else 0.0 * ones for a in range(comps)]) for b in range(comps)]

    def chain(block, other):
        return [times(block, column) for column in other]

    def join(first, second):
        return [a + b for a, b in zip(first, second)]

    def put(d, part, other):
        for b in range(comps):
            send_mr[d, pl.ds(part * 25 + b * comps, comps)] = other[b]

    def put_across(part, other):
        for b in range(comps):
            for a in range(comps):
                send_m2[pl.ds(part * 25 + a * comps + b, GROUP, stride=ROWS_M), :] = other[b][a]

    arrive(maps_a)
    arrive(maps_b)
    last = GROUP - 1
    ahead = held_map(0, 0)
    put(1, 0, ahead)
    for d in range(1, GROUP):
        ahead = chain(held_map(d, 0), ahead)
        if d < last:
            put(d + 1, 0, ahead)
    start_but(maps_p, 0)
    put_across(0, ahead)

    def prefix(d):
        return [send_mr[d, pl.ds(b * comps, comps)] for b in range(comps)]

    behind = held_map(last, 2)
    across_map = chain(held_map(last, 1), prefix(last))
    for d in range(last - 1, -1, -1):
        put(d, 1, across_map)
        put(d, 2, behind)
        own = held_map(d, 2)
        entering = chain(held_map(d, 1), prefix(d)) if d else held_map(0, 1)
        across_map = join(entering, chain(own, across_map))
        behind = chain(own, behind)
    put_across(1, across_map)
    put_across(2, behind)
    start(maps_2)
    start_but(maps_q, last)
    put(0, 0, same)
    put(last, 1, [0.0 * column for column in same])
    put(last, 2, same)
    keep_own(send_m2, recv_m2, ROWS_M)
    recv_mr[spot] = send_mr[spot]

    @pl.when(spot == 0)
    def _():
        for i in range(1, GROUP):
            recv_mr[i, pl.ds(0, 25)] = send_mr[0, pl.ds(0, 25)]

    @pl.when(spot == last)
    def _():
        for i in range(last):
            recv_mr[i, pl.ds(25, 50)] = send_mr[last, pl.ds(25, 50)]

    arrive(ends_1)

    def end(d, part):
        return recv_v1[d, pl.ds(part * comps, comps)]

    reach = [jnp.zeros((comps, quarter, lanes), F32), end(0, 0)]
    for d in range(1, GROUP):
        reach.append(end(d, 0) + times(held_map(d, 0), reach[d]))
    back = [None] * GROUP
    back[last] = reach[0]
    back[last - 1] = end(last, 1) + times(held_map(last, 1), reach[last])
    for d in range(last - 1, 0, -1):
        back[d - 1] = end(d, 1) + times(held_map(d, 1), reach[d]) + times(held_map(d, 2), back[d])
    west_out = end(0, 1) + times(held_map(0, 2), back[0])
    for c in range(comps):
        send_v2[pl.ds(c, GROUP, stride=ROWS_V), :] = reach[GROUP][c]
        send_v2[pl.ds(8 + c, GROUP, stride=ROWS_V), :] = west_out[c]
    start(ends_2)
    keep_own(send_v2, recv_v2, ROWS_V)
    for d in range(GROUP):
        send_r1[d, pl.ds(0, comps)] = reach[d]
        send_r1[d, pl.ds(comps, comps)] = back[d]
    start(back_1)
    recv_r1[spot] = send_r1[spot]

    def apply(start_row, vector):
        return total(
            recv_m2[pl.ds(start_row + b, comps, stride=comps), :] * vector[b:b + 1] for b in range(comps)
        )

    arrive(maps_2)
    arrive(ends_2)
    came = jnp.zeros((comps, lanes), F32)
    forward_in = []
    for i in range(GROUP):
        forward_in.append(came)
        send_r2[pl.ds(i * ROWS_V, comps), :] = came
        if i < GROUP - 1:
            came = recv_v2[pl.ds(i * ROWS_V, comps), :] + apply(i * ROWS_M, came)
    came = jnp.zeros((comps, lanes), F32)
    for i in range(GROUP - 1, -1, -1):
        send_r2[pl.ds(i * ROWS_V + 8, comps), :] = came
        if i > 0:
            came = (
                recv_v2[pl.ds(i * ROWS_V + 8, comps), :] + apply(i * ROWS_M + 25, forward_in[i])
                + apply(i * ROWS_M + 50, came)
            )
    start(back_2)
    recv_r2[aligned(mine * ROWS_V, ROWS_V), :] = send_r2[aligned(group * ROWS_V, ROWS_V), :]

    arrive_but(maps_p, 0)
    arrive_but(maps_q, last)
    arrive(back_1)
    arrive(back_2)
    parts = []
    for i in range(GROUP):
        into = [
            jnp.stack([
                recv_r2[pl.ds(i * quarter * ROWS_V + part * 8 + c, quarter, stride=ROWS_V), :] for c in range(comps)
            ])
            for part in range(2)
        ]
        block = [[recv_mr[i, pl.ds(part * 25 + b * comps, comps)] for b in range(comps)] for part in range(3)]
        forward_in = recv_r1[i, pl.ds(0, comps)] + times(block[0], into[0])
        backward_in = recv_r1[i, pl.ds(comps, comps)] + times(block[1], into[0]) + times(block[2], into[1])
        parts.append([forward_in[c] for c in range(comps)] + [backward_in[c] for c in range(comps)])
    came = [jnp.concatenate([part[c] for part in parts], axis=0) for c in range(2 * comps)]

    lax.fori_loop(0, planes, forward, came[:comps])

    def finish(turn, held):
        x = planes - 1 - turn
        held = backward(turn, held)
        for a in range(comps):
            upd[x, a] = held[a]
        return held

    lax.fori_loop(0, planes, finish, came[comps:])
    for copy in halos + maps_a + maps_b + maps_2 + ends_1 + ends_2 + back_2 + back_1:
        copy.wait_send()
    sent_but(maps_p, 0)
    sent_but(maps_q, last)


def on_device(n, ny, state_field, source, fluid_mask, cell_kind, boundary_side_number, center_matrix,
              flux_jacobian_blocks, wall_matrix, diag_inverse, lower_coupling, upper_neighbour_block):
    planes, comps, rows, lanes = state_field.shape
    assert n == GROUP * GROUP and rows == n and comps == 5 and planes % 2 == 0
    cells = comps * rows
    quarter = rows // GROUP
    vmem = pltpu.VMEM
    field = vmem((planes, comps, rows, lanes), F32)
    flags = vmem((planes * rows, lanes), jnp.int32)
    blocks = vmem((planes, comps, comps, rows, lanes), F32)
    maps = vmem((GROUP, MAPS, quarter, lanes), F32)
    ends = vmem((GROUP, 2 * comps, quarter, lanes), F32)
    maps_across = vmem((GROUP * ROWS_M, lanes), F32)
    ends_across = vmem((GROUP * ROWS_V, lanes), F32)
    hbm = pl.BlockSpec(memory_space=pltpu.HBM)
    matrix = pltpu.SMEM((comps, comps), F32)
    update, residual = pl.pallas_call(
        functools.partial(kernel, n, ny),
        out_shape=(
            pltpu.VMEM(state_field.shape, F32),
            pltpu.VMEM((planes * cells, lanes), F32),
        ),
        in_specs=[hbm] * 11,
        out_specs=(pl.BlockSpec(memory_space=pltpu.VMEM),) * 2,
        scratch_shapes=[
            matrix, pltpu.SMEM((comps, 6, comps), F32), matrix, matrix, matrix,
            field, field, flags, flags, flags, blocks,
            vmem(((planes + 2) * cells, lanes), F32),
            vmem((2, planes * comps, lanes), F32),
            vmem((2, planes * comps, lanes), F32),
            vmem((planes * cells, lanes), F32),
            blocks, blocks, blocks, field, field,
            maps, maps, ends, ends, ends, ends, maps, maps,
            maps_across, maps_across, ends_across, ends_across, ends_across, vmem((n * ROWS_V, lanes), F32),
            pltpu.SemaphoreType.DMA((11,)),
            pltpu.SemaphoreType.DMA((5,)), pltpu.SemaphoreType.DMA((5,)),
            pltpu.SemaphoreType.DMA((8, GROUP - 1)), pltpu.SemaphoreType.DMA((8, GROUP - 1)),
            pltpu.SemaphoreType.DMA((n - 1,)), pltpu.SemaphoreType.DMA((n - 1,)),
        ],
        compiler_params=pltpu.CompilerParams(
            collective_id=0, has_side_effects=True, vmem_limit_bytes=61 * 1024 * 1024
        ),
    )(
        state_field, source, *(a.reshape(planes * rows, lanes) for a in (fluid_mask, cell_kind, boundary_side_number)),
        diag_inverse, center_matrix, jnp.transpose(flux_jacobian_blocks, (1, 0, 2)), wall_matrix,
        lower_coupling, upper_neighbour_block,
    )
    return write(update, residual.reshape(state_field.shape))


def write_kernel(update, residual, update_out, residual_out, sems):
    copies = [
        pltpu.make_async_copy(update, update_out, sems.at[0]),
        pltpu.make_async_copy(residual, residual_out, sems.at[1]),
    ]
    for copy in copies:
        copy.start()
    for copy in copies:
        copy.wait()


def write(update, residual):
    return pl.pallas_call(
        write_kernel,
        out_shape=(jax.ShapeDtypeStruct(update.shape, F32), jax.ShapeDtypeStruct(residual.shape, F32)),
        in_specs=[pl.BlockSpec(memory_space=pltpu.VMEM)] * 2,
        out_specs=(pl.BlockSpec(memory_space=pltpu.HBM),) * 2,
        scratch_shapes=[pltpu.SemaphoreType.DMA((2,))],
        compiler_params=pltpu.CompilerParams(vmem_limit_bytes=1024 * 1024),
    )(update, residual)


def solution(mesh):
    field = P("gx", None, "gy", "gz")
    flags = P("gx", "gy", "gz")
    return jax.shard_map(
        functools.partial(on_device, mesh.shape["gx"], mesh.shape["gy"]),
        mesh=mesh,
        in_specs=(field, field, flags, flags, flags, P(), P(), P(), P("gx", None, None, "gy", "gz"), P(), P()),
        out_specs=(field, field),
        check_vma=False,
    )
```

```python
import functools

import jax
import jax.numpy as jnp
from jax import lax
from jax.experimental import pallas as pl
from jax.experimental.pallas import tpu as pltpu
from jax.sharding import PartitionSpec as P

MESH = pl.DeviceIdType.MESH
F32 = jnp.float32
GROUP = 4
MAPS = 75
ROWS_M = 80
CHUNKS = 4
ROWS_V = 16


def aligned(start, size):
    return pl.ds(pl.multiple_of(start, 8), size)


def total(terms):
    terms = list(terms)
    while len(terms) > 1:
        terms = [a + b for a, b in zip(terms[::2], terms[1::2])] + terms[len(terms) & ~1:]
    return terms[0]


def times(block, column):
    return total(part * column[b][None] for b, part in enumerate(block))


def kernel(
    n, ny,
    state_hbm, source_hbm, fluid_hbm, kind_hbm, side_hbm, diag_hbm,
    center_hbm, jac_hbm, wall_hbm, lower_hbm, upper_hbm,
    upd, res,
    center, jac, wall, lower, upper,
    state, source, fluid, kind, side, diag,
    masked, ysend, yrecv, zrecv,
    dl, du, tf, g, sw,
    send_m1, recv_m1, send_v1, recv_v1, send_r1, recv_r1, send_mr, recv_mr,
    send_m2, recv_m2, send_v2, recv_v2, send_r2, recv_r2,
    in_sem, halo_send, halo_recv, x_send, x_recv, line_send, line_recv,
):
    planes, comps, rows, lanes = state.shape
    cells = comps * rows
    quarter = rows // GROUP
    me = lax.axis_index("gx")
    my = lax.axis_index("gy")
    mz = lax.axis_index("gz")
    spot, group = lax.rem(me, GROUP), me // GROUP
    east, west = lax.rem(me + 1, n), lax.rem(me + n - 1, n)
    north, south = lax.rem(my + 1, ny), lax.rem(my + ny - 1, ny)
    in_group = [(p, me - spot + p) for p in (lax.rem(spot + k, GROUP) for k in range(1, GROUP))]
    line = [lax.rem(me + k, n) for k in range(1, n)]
    across = [(p, p * GROUP + spot) for p in (lax.rem(group + k, GROUP) for k in range(1, GROUP))]

    pairs = [
        (diag_hbm, diag), (state_hbm, state), (fluid_hbm, fluid), (source_hbm, source), (side_hbm, side), (kind_hbm, kind),
        (lower_hbm, lower), (upper_hbm, upper), (center_hbm, center), (wall_hbm, wall), (jac_hbm, jac),
    ]
    loads = [pltpu.make_async_copy(hbm, vmem, in_sem.at[i]) for i, (hbm, vmem) in enumerate(pairs)]
    barrier = pltpu.get_barrier_semaphore()
    for other in (north, south):
        pl.semaphore_signal(barrier, inc=1, device_id={"gy": other}, device_id_type=MESH)
    for peer in line:
        pl.semaphore_signal(barrier, inc=1, device_id={"gx": peer}, device_id_type=MESH)
    pl.semaphore_signal(barrier, inc=1, device_id={"gz": 1 - mz}, device_id_type=MESH)
    for i in (1, 2, 6, 7, 0, 8, 9, 10):
        loads[i].start()

    loads[1].wait()
    loads[2].wait()

    def mask_plane(x, _):
        keep = fluid[aligned(x * rows, rows), :].astype(F32)
        for c in range(comps):
            masked[aligned((x + 1) * cells + c * rows, rows), :] = state[x, c] * keep
        return 0

    lax.fori_loop(0, planes, mask_plane, 0)
    ysend[0] = masked[pl.ds(cells + rows - 1, planes * comps, stride=rows), :]
    ysend[1] = masked[pl.ds(cells, planes * comps, stride=rows), :]

    for i in (6, 7, 0):
        loads[i].wait()
    for i in range(3, 6):
        loads[i].start()

    def products(x, _):
        for a in range(comps):
            row = [diag[x, a, b] for b in range(comps)]
            for c in range(comps):
                dl[x, a, c] = total(row[b] * lower[b, c] for b in range(comps))
                du[x, a, c] = total(row[b] * upper[b, c] for b in range(comps))
        return 0

    lax.fori_loop(0, planes, products, 0)

    def columns(ref, x, half):
        return [ref[x, :, b, aligned(half * 8, 8), :] for b in range(comps)]

    def pack(part, half, held):
        for b in range(comps):
            for a in range(comps):
                for i in range(8 // quarter):
                    send_m1[half * (8 // quarter) + i, part * 25 + b * comps + a] = (
                        held[b][a, i * quarter:(i + 1) * quarter]
                    )

    def forward_maps(half):
        def step(x, held):
            block = columns(dl, x, half)
            held = [times(block, column) for column in held]
            for b in range(comps):
                tf[x, :, b, aligned(half * 8, 8), :] = held[b]
            return held

        first = columns(dl, 0, half)
        for b in range(comps):
            tf[0, :, b, aligned(half * 8, 8), :] = first[b]
        pack(0, half, lax.fori_loop(1, planes, step, first))


    def remote(src, dst, send_sem, recv_sem, where):
        return pltpu.make_async_remote_copy(
            src_ref=src, dst_ref=dst, send_sem=send_sem, recv_sem=recv_sem, device_id=where, device_id_type=MESH
        )

    halos = [
        remote(ysend.at[0], yrecv.at[0], halo_send.at[0], halo_recv.at[0], {"gy": north}),
        remote(ysend.at[1], yrecv.at[1], halo_send.at[1], halo_recv.at[1], {"gy": south}),
        remote(
            masked.at[pl.ds(planes * cells, cells)], masked.at[pl.ds(0, cells)],
            halo_send.at[2], halo_recv.at[2], {"gx": east},
        ),
        remote(
            masked.at[pl.ds(cells, cells)], masked.at[pl.ds((planes + 1) * cells, cells)],
            halo_send.at[3], halo_recv.at[3], {"gx": west},
        ),
        remote(masked.at[pl.ds(cells, planes * cells)], zrecv, halo_send.at[4], halo_recv.at[4], {"gz": 1 - mz}),
    ]

    def swap_in_group(src, dst, slot, part):
        return [
            remote(
                src.at[p, part], dst.at[spot, part], x_send.at[slot, k], x_recv.at[slot, k], {"gx": peer}
            )
            for k, (p, peer) in enumerate(in_group)
        ]

    def swap_across(src, dst, size, slot):
        return [
            remote(
                src.at[aligned(p * size, size)], dst.at[aligned(group * size, size)],
                x_send.at[slot, k], x_recv.at[slot, k], {"gx": peer},
            )
            for k, (p, peer) in enumerate(across)
        ]

    maps_a = swap_in_group(send_m1, recv_m1, 0, pl.ds(0, 25))
    maps_b = swap_in_group(send_m1, recv_m1, 1, pl.ds(25, 50))
    maps_2 = swap_across(send_m2, recv_m2, ROWS_M, 2)
    ends_1 = swap_in_group(send_v1, recv_v1, 3, pl.ds(0, 2 * comps))
    ends_2 = swap_across(send_v2, recv_v2, ROWS_V, 4)
    maps_p = swap_in_group(send_mr, recv_mr, 5, pl.ds(0, 25))
    maps_q = swap_in_group(send_mr, recv_mr, 7, pl.ds(25, 50))
    mine = spot * GROUP + group
    back_2 = [
        remote(
            send_r2.at[aligned(peer // GROUP * ROWS_V, ROWS_V)], recv_r2.at[aligned(mine * ROWS_V, ROWS_V)],
            line_send.at[k], line_recv.at[k], {"gx": peer},
        )
        for k, peer in enumerate(line)
    ]
    back_1 = swap_in_group(send_r1, recv_r1, 6, pl.ds(0, 2 * comps))

    def start(copies):
        for copy in copies:
            copy.start()

    def start_but(copies, skipped):
        for (p, _), copy in zip(in_group, copies):
            pl.when(p != skipped)(copy.start)

    def sent_but(copies, skipped):
        for (p, _), copy in zip(in_group, copies):
            pl.when(p != skipped)(copy.wait_send)

    def arrive_but(copies, skipped):
        for copy in copies:
            pl.when(spot != skipped)(copy.wait_recv)

    def arrive(copies):
        for copy in copies:
            copy.wait_recv()

    def keep_own(src, dst, size):
        dst[aligned(group * size, size), :] = src[aligned(group * size, size), :]

    pl.semaphore_wait(barrier, n + 2)
    start(halos)
    for half in range(rows // 8):
        forward_maps(half)
    start(maps_a)

    def backward_maps(half):
        def through(turn, held):
            x = planes - 2 - turn
            block = columns(du, x, half)
            return [tf[x, :, b, aligned(half * 8, 8), :] - times(block, held[b]) for b in range(comps)]

        def back(turn, held):
            x = planes - 2 - turn
            block = columns(du, x, half)
            return [-times(block, column) for column in held]

        pack(1, half, lax.fori_loop(0, planes - 1, through, columns(tf, planes - 1, half)))
        pack(2, half, lax.fori_loop(0, planes - 1, back, [-column for column in columns(du, planes - 1, half)]))

    for half in range(rows // 8):
        backward_maps(half)
    start(maps_b)
    recv_m1[spot] = send_m1[spot]

    arrive(halos[2:])
    masked[0:cells, :] = jnp.where(me == 0, 0.0, masked[0:cells, :])
    top = pl.ds((planes + 1) * cells, cells)
    masked[top, :] = jnp.where(me == n - 1, 0.0, masked[top, :])
    for i in (3, 4, 5, 8, 9, 10):
        loads[i].wait()

    row_id = lax.broadcasted_iota(jnp.int32, (rows, lanes), 0)
    lane_id = lax.broadcasted_iota(jnp.int32, (rows, lanes), 1)
    from_low = jnp.where(mz == 0, 0.0, 1.0).astype(F32)
    from_high = 1.0 - from_low

    def weights(flag, wet):
        return jnp.where(flag == 0, 1.0, jnp.where(flag == 1, 2.0, 4.0)) * wet.astype(F32)

    def residual_planes(step, _):
        xs = (2 * step, 2 * step + 1)
        sides = [side[aligned(x * rows, rows), :] for x in xs]
        flux = [[None] * comps for _ in xs]

        def add(matrix, b, values):
            for a in range(comps):
                weight = matrix(a, b)
                for i, value in enumerate(values):
                    term = weight * value
                    flux[i][a] = term if flux[i][a] is None else flux[i][a] + term

        for b in range(comps):
            own = [state[x, b] for x in xs]
            add(lambda a, b: center[a, b], b, own)
            add(lambda a, b: wall[a, b], b, [jnp.where(s < 6, v, 0.0) for s, v in zip(sides, own)])
            here = [masked[aligned((x + 1) * cells + b * rows, rows), :] for x in xs]
            other = [zrecv[aligned(x * cells + b * rows, rows), :] for x in xs]
            neighbours = [
                [masked[aligned(x * cells + b * rows, rows), :] for x in xs],
                [masked[aligned((x + 2) * cells + b * rows, rows), :] for x in xs],
                [pltpu.roll(v, 1, 0) for v in here],
                [pltpu.roll(v, rows - 1, 0) for v in here],
                [pltpu.roll(jnp.where(lane_id == lanes - 1, o * from_low, v), 1, 1) for o, v in zip(other, here)],
                [pltpu.roll(jnp.where(lane_id == 0, o * from_high, v), lanes - 1, 1) for o, v in zip(other, here)],
            ]
            edge = [None, None, 0, rows - 1, None, None]
            for d in range(6):
                closed = [s == d for s in sides]
                if edge[d] is not None:
                    closed = [jnp.logical_or(c, row_id == edge[d]) for c in closed]
                add(lambda a, b: jac[a, d, b], b, [jnp.where(c, 0.0, v) for c, v in zip(closed, neighbours[d])])
        for i, x in enumerate(xs):
            weight = weights(kind[aligned(x * rows, rows), :], fluid[aligned(x * rows, rows), :])
            for a in range(comps):
                res[aligned(x * cells + a * rows, rows), :] = (source[x, a] - flux[i][a]) * weight
        return 0

    lax.fori_loop(0, planes // 2, residual_planes, 0)

    arrive(halos[:2])
    for i, (d, row) in enumerate(((2, 0), (3, rows - 1))):
        edge_rows = pl.ds(row, planes, stride=rows)
        is_open = jnp.logical_and(side[edge_rows, :] != d, my != (0, ny - 1)[i])
        weight = jnp.where(is_open, weights(kind[edge_rows, :], fluid[edge_rows, :]), 0.0)
        beyond = [yrecv[i, pl.ds(b, planes, stride=comps), :] for b in range(comps)]
        for a in range(comps):
            at = pl.ds(a * rows + row, planes, stride=cells)
            res[at, :] = res[at, :] - weight * total(jac[a, d, b] * beyond[b] for b in range(comps))

    def first_forward(x, held):
        terms = [res[aligned(x * cells + b * rows, rows), :] for b in range(comps)]
        for a in range(comps):
            g[x, a] = total(diag[x, a, b] * terms[b] for b in range(comps))
        return forward(x, held)

    def forward(x, held):
        held = [
            g[x, a] + total(dl[x, a, b] * held[b] for b in range(comps)) for a in range(comps)
        ]
        for a in range(comps):
            sw[x, a] = held[a]
        return held

    def backward(turn, held):
        x = planes - 1 - turn
        return [
            sw[x, a] - total(du[x, a, b] * held[b] for b in range(comps)) for a in range(comps)
        ]

    zeros = [jnp.zeros((rows, lanes), F32)] * comps
    east_end = lax.fori_loop(0, planes, first_forward, zeros)
    west_end = lax.fori_loop(0, planes, backward, zeros)
    for c, value in enumerate(list(east_end) + list(west_end)):
        for i in range(GROUP):
            send_v1[i, c] = value[i * quarter:(i + 1) * quarter]
    start(ends_1)
    recv_v1[spot] = send_v1[spot]

    def held_map(d, part):
        return [recv_m1[d, pl.ds(part * 25 + b * comps, comps)] for b in range(comps)]

    ones = jnp.ones((quarter, lanes), F32)
    same = [jnp.stack([ones if a == b else 0.0 * ones for a in range(comps)]) for b in range(comps)]

    def chain(block, other):
        return [times(block, column) for column in other]

    def join(first, second):
        return [a + b for a, b in zip(first, second)]

    def put(d, part, other):
        for b in range(comps):
            send_mr[d, pl.ds(part * 25 + b * comps, comps)] = other[b]

    def put_across(part, other):
        for b in range(comps):
            for a in range(comps):
                send_m2[pl.ds(part * 25 + a * comps + b, GROUP, stride=ROWS_M), :] = other[b][a]

    arrive(maps_a)
    arrive(maps_b)
    last = GROUP - 1
    ahead = held_map(0, 0)
    put(1, 0, ahead)
    for d in range(1, GROUP):
        ahead = chain(held_map(d, 0), ahead)
        if d < last:
            put(d + 1, 0, ahead)
    start_but(maps_p, 0)
    put_across(0, ahead)

    def prefix(d):
        return [send_mr[d, pl.ds(b * comps, comps)] for b in range(comps)]

    behind = held_map(last, 2)
    across_map = chain(held_map(last, 1), prefix(last))
    for d in range(last - 1, -1, -1):
        put(d, 1, across_map)
        put(d, 2, behind)
        own = held_map(d, 2)
        entering = chain(held_map(d, 1), prefix(d)) if d else held_map(0, 1)
        across_map = join(entering, chain(own, across_map))
        behind = chain(own, behind)
    put_across(1, across_map)
    put_across(2, behind)
    start(maps_2)
    start_but(maps_q, last)
    put(0, 0, same)
    put(last, 1, [0.0 * column for column in same])
    put(last, 2, same)
    keep_own(send_m2, recv_m2, ROWS_M)
    recv_mr[spot] = send_mr[spot]

    @pl.when(spot == 0)
    def _():
        for i in range(1, GROUP):
            recv_mr[i, pl.ds(0, 25)] = send_mr[0, pl.ds(0, 25)]

    @pl.when(spot == last)
    def _():
        for i in range(last):
            recv_mr[i, pl.ds(25, 50)] = send_mr[last, pl.ds(25, 50)]

    arrive(ends_1)

    def end(d, part):
        return recv_v1[d, pl.ds(part * comps, comps)]

    reach = [jnp.zeros((comps, quarter, lanes), F32), end(0, 0)]
    for d in range(1, GROUP):
        reach.append(end(d, 0) + times(held_map(d, 0), reach[d]))
    back = [None] * GROUP
    back[last] = reach[0]
    back[last - 1] = end(last, 1) + times(held_map(last, 1), reach[last])
    for d in range(last - 1, 0, -1):
        back[d - 1] = end(d, 1) + times(held_map(d, 1), reach[d]) + times(held_map(d, 2), back[d])
    west_out = end(0, 1) + times(held_map(0, 2), back[0])
    for c in range(comps):
        send_v2[pl.ds(c, GROUP, stride=ROWS_V), :] = reach[GROUP][c]
        send_v2[pl.ds(8 + c, GROUP, stride=ROWS_V), :] = west_out[c]
    start(ends_2)
    keep_own(send_v2, recv_v2, ROWS_V)
    for d in range(GROUP):
        send_r1[d, pl.ds(0, comps)] = reach[d]
        send_r1[d, pl.ds(comps, comps)] = back[d]
    start(back_1)
    recv_r1[spot] = send_r1[spot]

    def apply(start_row, vector):
        return total(
            recv_m2[pl.ds(start_row + b, comps, stride=comps), :] * vector[b:b + 1] for b in range(comps)
        )

    arrive(maps_2)
    arrive(ends_2)
    came = jnp.zeros((comps, lanes), F32)
    forward_in = []
    for i in range(GROUP):
        forward_in.append(came)
        send_r2[pl.ds(i * ROWS_V, comps), :] = came
        if i < GROUP - 1:
            came = recv_v2[pl.ds(i * ROWS_V, comps), :] + apply(i * ROWS_M, came)
    came = jnp.zeros((comps, lanes), F32)
    for i in range(GROUP - 1, -1, -1):
        send_r2[pl.ds(i * ROWS_V + 8, comps), :] = came
        if i > 0:
            came = (
                recv_v2[pl.ds(i * ROWS_V + 8, comps), :] + apply(i * ROWS_M + 25, forward_in[i])
                + apply(i * ROWS_M + 50, came)
            )
    start(back_2)
    recv_r2[aligned(mine * ROWS_V, ROWS_V), :] = send_r2[aligned(group * ROWS_V, ROWS_V), :]

    arrive_but(maps_p, 0)
    arrive_but(maps_q, last)
    arrive(back_1)
    arrive(back_2)
    parts = []
    for i in range(GROUP):
        into = [
            jnp.stack([
                recv_r2[pl.ds(i * quarter * ROWS_V + part * 8 + c, quarter, stride=ROWS_V), :] for c in range(comps)
            ])
            for part in range(2)
        ]
        block = [[recv_mr[i, pl.ds(part * 25 + b * comps, comps)] for b in range(comps)] for part in range(3)]
        forward_in = recv_r1[i, pl.ds(0, comps)] + times(block[0], into[0])
        backward_in = recv_r1[i, pl.ds(comps, comps)] + times(block[1], into[0]) + times(block[2], into[1])
        parts.append([forward_in[c] for c in range(comps)] + [backward_in[c] for c in range(comps)])
    came = [jnp.concatenate([part[c] for part in parts], axis=0) for c in range(2 * comps)]

    lax.fori_loop(0, planes, forward, came[:comps])

    def finish(turn, held):
        x = planes - 1 - turn
        held = backward(turn, held)
        for a in range(comps):
            upd[x, a] = held[a]
        return held

    lax.fori_loop(0, planes, finish, came[comps:])
    for copy in halos + maps_a + maps_b + maps_2 + ends_1 + ends_2 + back_2 + back_1:
        copy.wait_send()
    sent_but(maps_p, 0)
    sent_but(maps_q, last)


def on_device(n, ny, state_field, source, fluid_mask, cell_kind, boundary_side_number, center_matrix,
              flux_jacobian_blocks, wall_matrix, diag_inverse, lower_coupling, upper_neighbour_block):
    planes, comps, rows, lanes = state_field.shape
    assert n == GROUP * GROUP and rows == n and comps == 5 and planes % 2 == 0
    cells = comps * rows
    quarter = rows // GROUP
    vmem = pltpu.VMEM
    field = vmem((planes, comps, rows, lanes), F32)
    flags = vmem((planes * rows, lanes), jnp.int32)
    blocks = vmem((planes, comps, comps, rows, lanes), F32)
    maps = vmem((GROUP, MAPS, quarter, lanes), F32)
    ends = vmem((GROUP, 2 * comps, quarter, lanes), F32)
    maps_across = vmem((GROUP * ROWS_M, lanes), F32)
    ends_across = vmem((GROUP * ROWS_V, lanes), F32)
    hbm = pl.BlockSpec(memory_space=pltpu.HBM)
    matrix = pltpu.SMEM((comps, comps), F32)
    update, residual = pl.pallas_call(
        functools.partial(kernel, n, ny),
        out_shape=(
            pltpu.VMEM(state_field.shape, F32),
            pltpu.VMEM((planes * cells, lanes), F32),
        ),
        in_specs=[hbm] * 11,
        out_specs=(pl.BlockSpec(memory_space=pltpu.VMEM),) * 2,
        scratch_shapes=[
            matrix, pltpu.SMEM((comps, 6, comps), F32), matrix, matrix, matrix,
            field, field, flags, flags, flags, blocks,
            vmem(((planes + 2) * cells, lanes), F32),
            vmem((2, planes * comps, lanes), F32),
            vmem((2, planes * comps, lanes), F32),
            vmem((planes * cells, lanes), F32),
            blocks, blocks, blocks, field, field,
            maps, maps, ends, ends, ends, ends, maps, maps,
            maps_across, maps_across, ends_across, ends_across, ends_across, vmem((n * ROWS_V, lanes), F32),
            pltpu.SemaphoreType.DMA((11,)),
            pltpu.SemaphoreType.DMA((5,)), pltpu.SemaphoreType.DMA((5,)),
            pltpu.SemaphoreType.DMA((8, GROUP - 1)), pltpu.SemaphoreType.DMA((8, GROUP - 1)),
            pltpu.SemaphoreType.DMA((n - 1,)), pltpu.SemaphoreType.DMA((n - 1,)),
        ],
        compiler_params=pltpu.CompilerParams(
            collective_id=0, has_side_effects=True, vmem_limit_bytes=61 * 1024 * 1024
        ),
    )(
        state_field, source, *(a.reshape(planes * rows, lanes) for a in (fluid_mask, cell_kind, boundary_side_number)),
        diag_inverse, center_matrix, jnp.transpose(flux_jacobian_blocks, (1, 0, 2)), wall_matrix,
        lower_coupling, upper_neighbour_block,
    )
    return write(update, residual.reshape(state_field.shape))


def write_kernel(update, residual, update_out, residual_out, sems):
    size = update.shape[0] // CHUNKS
    copies = [
        pltpu.make_async_copy(src.at[pl.ds(i * size, size)], dst.at[pl.ds(i * size, size)], sems.at[k, i])
        for k, (src, dst) in enumerate(((update, update_out), (residual, residual_out)))
        for i in range(CHUNKS)
    ]
    for copy in copies:
        copy.start()
    for copy in copies:
        copy.wait()


def write(update, residual):
    return pl.pallas_call(
        write_kernel,
        out_shape=(jax.ShapeDtypeStruct(update.shape, F32), jax.ShapeDtypeStruct(residual.shape, F32)),
        in_specs=[pl.BlockSpec(memory_space=pltpu.VMEM)] * 2,
        out_specs=(pl.BlockSpec(memory_space=pltpu.HBM),) * 2,
        scratch_shapes=[pltpu.SemaphoreType.DMA((2, CHUNKS))],
        compiler_params=pltpu.CompilerParams(vmem_limit_bytes=1024 * 1024),
    )(update, residual)


def solution(mesh):
    field = P("gx", None, "gy", "gz")
    flags = P("gx", "gy", "gz")
    return jax.shard_map(
        functools.partial(on_device, mesh.shape["gx"], mesh.shape["gy"]),
        mesh=mesh,
        in_specs=(field, field, flags, flags, flags, P(), P(), P(), P("gx", None, None, "gy", "gz"), P(), P()),
        out_specs=(field, field),
        check_vma=False,
    )
```
